256 devices in a mesh: tilt: 8 (over z), tile: 32 (over x, y, core).
Axes of the slice: x: 4, y: 4, z: 8, core: 2. Of those that a mesh axis runs over, the one named last changes fastest.
Arguments:
- volumes: bfloat16 [192, 128, 64, 128], P('tile', 'tilt'), may hold values from -0.75 to 0.75
- angles: float32 [16], replicated, may hold values from -1.05 to 1.05
- defocus: float32 [16], P('tilt'), may hold values from 0.01 to 0.1
- row_offsets: int32 [192, 16], P('tile', 'tilt'), may hold values from 0 to 4095, as said below
- col_offsets: int32 [192, 16], P('tile', 'tilt'), may hold values from 0 to 128
- measured: float32 [16, 4096, 256], P('tilt', 'tile'), may hold values from -6 to 6
Outputs:
- residual: float32 [16, 4096, 256], P('tilt', 'tile')
- volume_step: float32 [192, 128, 64, 128], P('tile', 'tilt')
The draws below stay inside these ranges and needn't reach their ends.
Inputs may be any that keep to these rules, and one draw needn't show every extreme that they name: row_offsets[b, t] // 128 is the strip that holds the window's top row. Among the 6 boxes of one index of tile and the 2 tilts of one index of tilt, at most 2 windows have their top row in the same strip; in every draw, for every index of tilt, one strip receives exactly 2 such windows from every index of tile.
All inputs are finite; a program needn't handle non-finite values.
Results may differ from the reference program's by a relative error of at most 0.0047.
Values may be sent and summed in bfloat16 or wider, within the bound.
A program may use at most 64 MiB of HBM per device.

```python
import math
import jax
import jax.numpy as jnp
from jax import lax

BY = 128
BX = 128
BZ = 64
HR = 8
TILT_DEV = 2
BOX_DEV = 6
STRIP = 128
IMG_W = 256
TILTS = 16
BOXES = 192
IMG_H = 4096
CAP = 2


def draw_row_offsets(key, part):
    tile_count = BOXES // BOX_DEV
    group_count = TILTS // TILT_DEV
    item_count = BOX_DEV * TILT_DEV
    hot_key, block_key, offset_key = jax.random.split(jax.random.fold_in(key, 17), 3)
    busiest = jax.random.randint(hot_key, (group_count,), 0, tile_count, dtype=jnp.int32)
    others = (busiest[:, None] + 1 + jnp.arange((tile_count - 1) * CAP, dtype=jnp.int32)[None, :] // CAP) % tile_count
    block_keys = jax.random.split(block_key, tile_count * group_count)

    def one_block(block_seed, group_index):
        order_key, pick_key = jax.random.split(block_seed)
        item_order = jax.random.permutation(order_key, item_count)
        picked = jax.random.permutation(pick_key, others[group_index])[:item_count - CAP]
        ordered = jnp.concatenate([jnp.full((CAP,), busiest[group_index], jnp.int32), picked.astype(jnp.int32)])
        return jnp.zeros((item_count,), jnp.int32).at[item_order].set(ordered)
    group_of = jnp.tile(jnp.arange(group_count, dtype=jnp.int32), tile_count)
    targets = jax.vmap(one_block)(block_keys, group_of)
    targets = targets.reshape(tile_count, group_count, TILT_DEV, BOX_DEV).transpose(0, 3, 1, 2).reshape(BOXES, TILTS)
    within = jax.random.randint(offset_key, (BOXES, TILTS), 0, STRIP, dtype=jnp.int32)
    return targets * STRIP + within


def place_ends(entries, stream_key, least, largest):
    spot = [jax.random.randint(jax.random.fold_in(stream_key, axis), (), 0, length) for axis, length in enumerate(entries.shape)]
    main_axis = entries.shape.index(max(entries.shape))
    next_to = spot[:main_axis] + [(spot[main_axis] + 1) % entries.shape[main_axis]] + spot[main_axis + 1:]
    return entries.at[tuple(spot)].set(least).at[tuple(next_to)].set(largest)


def block_scale(key, dims, shards, smallest, largest):
    gain, own = 1.0, jax.random.fold_in(key, 6)
    for axis_at, parts in shards:
        heights = jnp.exp(jax.random.uniform(jax.random.fold_in(own, axis_at), (parts,), jnp.float32, smallest / len(shards), largest / len(shards)))
        gain = gain * jnp.repeat(heights, dims[axis_at] // parts).reshape([-1 if axis == axis_at else 1 for axis in range(len(dims))])
    return gain


def scatter_about(own_key, dims, deviation, reach, shards=(), kind=jnp.bfloat16):
    values = jax.random.normal(own_key, dims, jnp.float32) * deviation
    if len(shards) > 0:
        values = block_scale(own_key, dims, shards, -0.22, 0.18) * values
    return jnp.clip(values, min=-reach, max=reach).astype(kind)


def setup_inputs(seed: int = 0) -> dict:
    seeds = jax.random.split(jax.random.key(seed), 7)
    volumes = scatter_about(seeds[0], (BOXES, BY, BZ, BX), 0.125, 0.75, ((0, 32), (1, 8)))
    angles = jnp.clip(jax.random.uniform(seeds[1], (TILTS,), jnp.float32, -1.05, 1.05), -1.05, 1.05)
    defocus = jnp.clip(jnp.exp(math.log(0.1) - 2.3025851 * jax.random.uniform(seeds[2], (TILTS,), jnp.float32) ** block_scale(seeds[2], (TILTS,), ((0, 8),), -0.2, 0.2)), 0.01, 0.1)
    row_offsets = draw_row_offsets(jax.random.fold_in(seeds[6], 71), 0)
    col_offsets = place_ends(jax.random.randint(seeds[4], (BOXES, TILTS), 0, IMG_W - BX + 1), jax.random.fold_in(seeds[4], 1), 0, IMG_W - BX).astype(jnp.int32)
    measured = scatter_about(seeds[5], (TILTS, IMG_H, IMG_W), 1.0, 6.0, ((0, 8), (1, 32)), jnp.float32)
    return dict(volumes=volumes, angles=angles, defocus=defocus, row_offsets=row_offsets, col_offsets=col_offsets, measured=measured)


def shear_shift(tilt_angle, depth_values, box_depth):
    return (depth_values - (box_depth - 1) / 2.0) * jnp.sin(tilt_angle)


def tap_weight(offset, layer_shift):
    return jnp.maximum(0.0, 1.0 - jnp.abs(offset - layer_shift))


def point_spread(rho_sq, defocus, radius):
    spread_scale = float(radius * radius)
    return jnp.exp(-rho_sq / (2.0 * spread_scale)) * jnp.cos(defocus * rho_sq) / spread_scale


def rounded_weights(lower_tap, shifts):
    near_half = lax.optimization_barrier(tap_weight(lower_tap, shifts).astype(jnp.bfloat16))
    far_half = lax.optimization_barrier(tap_weight(lower_tap + 1.0, shifts).astype(jnp.bfloat16))
    return near_half.astype(jnp.float32), far_half.astype(jnp.float32)


def project_boxes(volumes, angles):
    margin = BZ // 2 + 2
    layers = jnp.pad(volumes, ((0, 0), (0, 0), (0, 0), (margin, margin))).transpose(2, 0, 1, 3)
    depth_values = jnp.arange(BZ, dtype=jnp.float32)

    def one_tilt(tilt_angle):
        shifts = shear_shift(tilt_angle, depth_values, BZ)
        lower_tap = jnp.floor(shifts)
        near_weight, far_weight = rounded_weights(lower_tap, shifts)
        starts = (margin - lower_tap).astype(jnp.int32)

        def add_layer(summed, inputs):
            depth_layer, begin_column, near_scale, far_scale = inputs
            near_layer = lax.dynamic_slice_in_dim(depth_layer, begin_column, BX, 2).astype(jnp.float32)
            far_layer = lax.dynamic_slice_in_dim(depth_layer, begin_column - 1, BX, 2).astype(jnp.float32)
            return summed + near_scale * near_layer + far_scale * far_layer, None

        summed, _ = lax.scan(add_layer, jnp.zeros((BOXES, BY, BX), jnp.float32), (layers, starts, near_weight, far_weight))
        return summed.astype(jnp.bfloat16)

    return lax.map(one_tilt, angles)


def back_project(back_windows, angles):
    margin = BZ // 2 + 2
    padded = jnp.pad(back_windows, ((0, 0), (0, 0), (0, 0), (margin, margin)))

    def one_layer(depth_value):
        shifts = shear_shift(angles, depth_value, BZ)
        lower_tap = jnp.floor(shifts)
        near_weight, far_weight = rounded_weights(lower_tap, shifts)
        starts = (margin + lower_tap).astype(jnp.int32)

        def add_tilt(summed, inputs):
            window_set, begin_column, near_scale, far_scale = inputs
            near_layer = lax.dynamic_slice_in_dim(window_set, begin_column, BX, 2).astype(jnp.float32)
            far_layer = lax.dynamic_slice_in_dim(window_set, begin_column + 1, BX, 2).astype(jnp.float32)
            return summed + near_scale * near_layer + far_scale * far_layer, None

        summed, _ = lax.scan(add_tilt, jnp.zeros((BOXES, BY, BX), jnp.float32), (padded, starts, near_weight, far_weight))
        return summed

    layers = lax.map(one_layer, jnp.arange(BZ, dtype=jnp.float32))
    return layers.transpose(1, 2, 0, 3) * (1.0 / TILTS)


def convolve(image_field, spread):
    result = lax.conv_general_dilated(
        image_field.astype(jnp.float32)[None],
        spread.astype(jnp.float32)[:, None],
        (1, 1),
        ((HR, HR), (HR, HR)),
        dimension_numbers=("NCHW", "OIHW", "NCHW"),
        feature_group_count=TILTS,
        precision=lax.Precision.HIGHEST,
    )
    return result[0]


def reference(volumes, angles, defocus, row_offsets, col_offsets, measured):
    windows = project_boxes(volumes, angles)
    canvas = jnp.zeros((TILTS, IMG_H + BY, IMG_W), jnp.float32)

    def place_item(item_index, current):
        tilt_index = (item_index // BOXES).astype(jnp.int32)
        box_index = (item_index % BOXES).astype(jnp.int32)
        corner = (tilt_index, row_offsets[box_index, tilt_index].astype(jnp.int32), col_offsets[box_index, tilt_index].astype(jnp.int32))
        patch_values = lax.dynamic_slice(current, corner, (1, BY, BX))
        return lax.dynamic_update_slice(current, patch_values + windows[tilt_index, box_index][None].astype(jnp.float32), corner)

    canvas = lax.fori_loop(0, TILTS * BOXES, place_item, canvas)
    predicted = canvas[:, :IMG_H].astype(jnp.bfloat16)
    offsets = jnp.arange(-HR, HR + 1, dtype=jnp.float32)
    rho_sq = offsets[:, None] ** 2 + offsets[None, :] ** 2
    spread = point_spread(rho_sq[None], defocus[:, None, None], HR).astype(jnp.bfloat16)
    residual = measured - convolve(predicted, spread)
    back_half = convolve(residual.astype(jnp.bfloat16), spread).astype(jnp.bfloat16)
    extended = jnp.concatenate([back_half, jnp.zeros((TILTS, BY, IMG_W), jnp.bfloat16)], axis=1)

    def cut_tilt(tilt_index, rows_here, columns_here):
        def cut_box(row_start, column_start):
            return lax.dynamic_slice(extended, (tilt_index, row_start.astype(jnp.int32), column_start.astype(jnp.int32)), (1, BY, BX))[0]

        return jax.vmap(cut_box)(rows_here, columns_here)

    back_windows = jax.vmap(cut_tilt)(jnp.arange(TILTS, dtype=jnp.int32), row_offsets.T, col_offsets.T)
    return residual, back_project(back_windows, angles)
```

```python
import functools

import jax
import jax.numpy as jnp
from jax import lax
from jax.experimental import pallas as pl
from jax.experimental.pallas import tpu as pltpu
from jax.sharding import PartitionSpec as P

HR = 8
MESH = pl.DeviceIdType.MESH
BF16 = jnp.bfloat16
F32 = jnp.float32
MIB = 1 << 20


def signal(device):
    pl.semaphore_signal(
        pltpu.get_barrier_semaphore(), inc=1, device_id=device, device_id_type=MESH
    )


def remote(src, dst, send_sem, recv_sem, device):
    return pltpu.make_async_remote_copy(
        src_ref=src, dst_ref=dst, send_sem=send_sem, recv_sem=recv_sem,
        device_id=device, device_id_type=MESH,
    )


def offsets_c_minus_x(transposed):
    rows = lax.broadcasted_iota(jnp.int32, (128, 128), 0)
    cols = lax.broadcasted_iota(jnp.int32, (128, 128), 1)
    return ((rows - cols) if transposed else (cols - rows)).astype(F32).astype(BF16)


def shear_block(tap, near, far, tilt, layer, apart):
    low = jnp.full((128, 128), tap[tilt, layer], F32).astype(BF16)
    high = jnp.full((128, 128), tap[tilt, layer] + 1.0, F32).astype(BF16)
    first = jnp.full((128, 128), near[tilt, layer], F32).astype(BF16)
    second = jnp.full((128, 128), far[tilt, layer], F32).astype(BF16)
    zero = jnp.zeros((128, 128), BF16)
    return jnp.where(apart == low, first, jnp.where(apart == high, second, zero))


def shear_tile(tap, near, far, tilt, layer, apart, transposed):
    make = lambda t, z: shear_block(tap, near, far, tilt + t, layer + z, apart)
    if transposed:
        parts = [[make(t, z) for z in range(2)] for t in range(2)]
    else:
        parts = [[make(t, z) for t in range(2)] for z in range(2)]
    return jnp.concatenate([jnp.concatenate(row, axis=1) for row in parts], axis=0)


def project_kernel(groups, tap, near, far, v_ref, out_ref, wide, pairs, sent, send_sems, recv_sems):
    me, tile = lax.axis_index("tilt"), lax.axis_index("tile")
    for d in range(1, groups):
        signal(((me + d) % groups, tile))
    rows = v_ref.shape[0]
    lines = rows // 64

    def widen(i, carry):
        at = pl.ds(pl.multiple_of(i * 512, 512), 512)
        wide[at, :] = v_ref[at, :].astype(F32)
        return carry

    lax.fori_loop(0, rows // 512, widen, 0)

    def gather(k, carry):
        even = wide[pl.ds(2 * k, lines, stride=64), :]
        odd = wide[pl.ds(2 * k + 1, lines, stride=64), :]
        pairs[k] = jnp.concatenate([even, odd], axis=1).astype(BF16)
        return carry

    lax.fori_loop(0, 32, gather, 0)
    pl.semaphore_wait(pltpu.get_barrier_semaphore(), groups - 1)
    apart = offsets_c_minus_x(False)
    copies = []
    for step in range(groups):
        d = 4 + step // 2 if step % 2 == 0 else 4 - (step + 1) // 2
        target = (me + d) % groups

        def add(k, acc):
            tile_w = shear_tile(tap, near, far, 2 * target, 2 * k, apart, False)
            return acc + jnp.dot(pairs[k], tile_w, preferred_element_type=F32)

        acc = lax.fori_loop(0, 32, add, jnp.zeros((lines, 256), F32), unroll=2)
        both = [acc[:, 128 * t : 128 * t + 128].astype(BF16).reshape(lines // 16, 16, 128) for t in range(2)]
        mine = pl.ds(pl.multiple_of(16 * me, 16), 16)
        if d == 0:
            for t in range(2):
                out_ref[t, :, mine, :] = both[t]
        else:
            for t in range(2):
                sent[step, t] = both[t]
            copy = remote(
                sent.at[step], out_ref.at[:, :, mine, :], send_sems.at[step], recv_sems.at[step], (target, tile)
            )
            copy.start()
            copies.append(copy)
    for copy in copies:
        copy.wait()


def place_kernel(rows_ref, cols_ref, w_ref, out_ref, canvas):
    tilts, boxes = w_ref.shape[:2]
    strips = out_ref.shape[1]

    def clear(i, carry):
        at = pl.ds(pl.multiple_of(i * 136, 8), 136)
        for t in range(tilts):
            canvas[t, at, :] = jnp.zeros((136, 256), F32)
        return carry

    lax.fori_loop(0, canvas.shape[1] // 136, clear, 0)
    for b in range(boxes):
        for t in range(tilts):
            row, col = rows_ref[b, t], cols_ref[b, t]
            window = jnp.concatenate([w_ref[t, b].astype(F32), jnp.zeros((128, 128), F32)], axis=1)
            window = pltpu.roll(window, col, 1)
            window = jnp.concatenate([window, jnp.zeros((8, 256), F32)], axis=0)
            window = pltpu.roll(window, row % 8, 0)
            at = pl.ds(pl.multiple_of(row // 8 * 8, 8), 136)
            canvas[t, at, :] = canvas[t, at, :] + window

    def narrow(i, carry):
        at = pl.ds(pl.multiple_of(i * 128, 128), 128)
        for t in range(tilts):
            out_ref[t, i] = canvas[t, at, :].astype(BF16)
        return carry

    lax.fori_loop(0, strips, narrow, 0)


def image_kernel(
    spread, can, measured, residual, img,
    r_a, s_b, o_b, f_b, s_c, o_c, f_c, own, table, pred_half, pred, halo, m_halo, res,
    a_sems, b_sems, c_sems, h_sems, g_sems,
):
    z, tile = lax.axis_index("tilt"), lax.axis_index("tile")
    x, y, c = tile // 8, (tile // 2) % 4, tile % 2
    other = 1 - c

    def dev(dx, dy):
        return (z, ((x + dx) % 4) * 8 + ((y + dy) % 4) * 2 + c)

    sibling = (z, x * 8 + y * 2 + other)
    below, above = (z, (tile + 1) % 32), (z, (tile + 31) % 32)
    right = lambda axis: dev(1, 0) if axis == 0 else dev(0, 1)
    left = lambda axis: dev(3, 0) if axis == 0 else dev(0, 3)
    place = (x, y)
    for device in (sibling, below, above, right(0), left(0), right(1), left(1)):
        signal(device)
    pl.semaphore_wait(pltpu.get_barrier_semaphore(), 7)

    steps = (2, 1, 3, 0)

    def block(ref, t, p, core):
        return ref.at[0, p, :, core] if t == 0 else ref.at[1, :, p, core]

    a_copies = {}
    for k, d in enumerate(steps):
        for t in range(2):
            p = (place[t] + d) % 4
            copy = remote(
                block(can, t, p, other), r_a.at[t, k], a_sems.at[0, t, k], a_sems.at[1, t, k], sibling
            )
            copy.start()
            a_copies[t, k] = copy
    m_copies = []
    for k, (device, start) in enumerate(((below, 120), (above, 0))):
        copy = remote(
            measured.at[:, pl.ds(start, 8), :], m_halo.at[k], h_sems.at[0, k], h_sems.at[1, k], device
        )
        copy.start()
        m_copies.append(copy)

    def fill(i, carry):
        lanes = lax.broadcasted_iota(jnp.int32, (16, 256), 1)
        subs = lax.broadcasted_iota(jnp.int32, (16, 256), 0) + i * 16
        apart = jnp.abs(lanes - subs).astype(F32).astype(BF16)
        masks = [apart == jnp.full((16, 256), j, F32).astype(BF16) for j in range(HR + 1)]
        for t in range(2):
            for a in range(HR + 1):
                value = jnp.zeros((16, 256), BF16)
                for j in range(HR + 1):
                    value = jnp.where(masks[j], jnp.full((16, 256), spread[t, a * (HR + 1) + j], F32).astype(BF16), value)
                table[t, a, pl.ds(pl.multiple_of(i * 16, 16), 16), :] = value
        return carry

    lax.fori_loop(0, 16, fill, 0)

    pending = []

    def go(src, dst, sems, t, k, device):
        copy = remote(src, dst, sems.at[0, t, k], sems.at[1, t, k], device)
        copy.start()
        pending.append(copy)
        return copy

    def local_b(t, k, half):
        d = steps[k]
        p = (place[t] + d) % 4
        at = pl.ds(2 * half, 2)
        mine = can[0, p, at, c] if t == 0 else can[1, at, p, c]
        return mine.astype(F32) + r_a[t, k, at].astype(F32)

    b_in = {}
    for t in range(2):
        a_copies[t, 0].wait_recv()
        for h, device in ((0, right(t)), (1, left(t))):
            s_b[t, 0, pl.ds(2 * h, 2)] = local_b(t, 0, h).astype(BF16)
            b_in[t, "opp", h] = go(s_b.at[t, 0, pl.ds(2 * h, 2)], o_b.at[t, h], b_sems, t, h, device)
    for t in range(2):
        for k, h, device in ((1, 1, right(t)), (2, 0, left(t))):
            a_copies[t, k].wait_recv()
            at = pl.ds(2 * h, 2)
            s_b[t, k, at] = local_b(t, k, h).astype(BF16)
            b_in[t, "free", k] = go(s_b.at[t, k, at], f_b.at[t, k - 1, at], b_sems, t, 1 + k, device)
    for t in range(2):
        for k, h, device in ((1, 0, right(t)), (2, 1, left(t))):
            at = pl.ds(2 * h, 2)
            b_in[t, "opp", h].wait_recv()
            s_b[t, k, at] = (local_b(t, k, h) + o_b[t, h].astype(F32)).astype(BF16)
            b_in[t, "bound", k] = go(s_b.at[t, k, at], f_b.at[t, k - 1, at], b_sems, t, 3 + k, device)
    for t in range(2):
        a_copies[t, 3].wait_recv()
        for h in range(2):
            own[t, pl.ds(2 * h, 2)] = local_b(t, 3, h)
        for k in (1, 2):
            b_in[t, "free", k].wait_recv()
            b_in[t, "bound", k].wait_recv()

    def local_c(t, k, half):
        q = (place[1 - t] + steps[k]) % 4
        at = pl.ds(64 * half, 64)
        return own[t, q, at, :] + f_b[t, 0, q, at, :].astype(F32) + f_b[t, 1, q, at, :].astype(F32)

    c_in = {}
    for t in range(2):
        for h, device in ((0, right(1 - t)), (1, left(1 - t))):
            at = pl.ds(64 * h, 64)
            s_c[t, 0, at] = local_c(t, 0, h).astype(BF16)
            c_in[t, "opp", h] = go(s_c.at[t, 0, at], o_c.at[t, h], c_sems, t, h, device)
        for k, h, device in ((1, 1, right(1 - t)), (2, 0, left(1 - t))):
            at = pl.ds(64 * h, 64)
            s_c[t, k, at] = local_c(t, k, h).astype(BF16)
            c_in[t, "free", k] = go(s_c.at[t, k, at], f_c.at[t, k - 1, at], c_sems, t, 1 + k, device)
    for t in range(2):
        for k, h, device in ((1, 0, right(1 - t)), (2, 1, left(1 - t))):
            at = pl.ds(64 * h, 64)
            c_in[t, "opp", h].wait_recv()
            s_c[t, k, at] = (local_c(t, k, h) + o_c[t, h].astype(F32)).astype(BF16)
            c_in[t, "bound", k] = go(s_c.at[t, k, at], f_c.at[t, k - 1, at], c_sems, t, 3 + k, device)
    for t in range(2):
        for k in (1, 2):
            c_in[t, "free", k].wait_recv()
            c_in[t, "bound", k].wait_recv()
        total = jnp.concatenate([local_c(t, 3, h) for h in range(2)], axis=0)
        total = total + f_c[t, 0].astype(F32) + f_c[t, 1].astype(F32)
        pred_half[t] = total.astype(BF16)
        pred[t, pl.ds(16, 128), :] = pred_half[t].astype(F32)

    p_copies = []
    for k, (device, start) in enumerate(((below, 112), (above, 0))):
        copy = remote(
            pred_half.at[:, pl.ds(start, 16), :], halo.at[k], h_sems.at[0, 2 + k], h_sems.at[1, 2 + k], device
        )
        copy.start()
        p_copies.append(copy)
    has_above = jnp.where(tile > 0, 1.0, 0.0).astype(F32)
    has_below = jnp.where(tile < 31, 1.0, 0.0).astype(F32)
    for copy in m_copies + p_copies:
        copy.wait_recv()
    for t in range(2):
        pred[t, pl.ds(0, 16), :] = halo[0, t].astype(F32) * has_above
        pred[t, pl.ds(144, 16), :] = halo[1, t].astype(F32) * has_below

    g_in = {}

    def give(t, bx, by, core, rows, k, device):
        at = pl.ds(rows[0], rows[1])
        where = img.at[t, bx, by, core, at]
        copy = remote(where, where, g_sems.at[0, t, k], g_sems.at[1, t, k], device)
        copy.start()
        pending.append(copy)
        return copy

    def at_place(t, p, q):
        return (p, q) if t == 0 else (q, p)

    for t in range(2):
        total = jnp.zeros((144, 256), F32)
        for i in range(2 * HR + 1):
            lhs = pred[t, pl.ds(i, 144), :].astype(BF16)
            total = total + jnp.dot(lhs, table[t, abs(i - HR)], preferred_element_type=F32)
        inner = measured[t] - total[8:136]
        residual[t] = inner
        res[t, pl.ds(8, 128), :] = inner.astype(BF16).astype(F32)
        res[t, pl.ds(0, 8), :] = (m_halo[0, t] - total[0:8]).astype(BF16).astype(F32) * has_above
        res[t, pl.ds(136, 8), :] = (m_halo[1, t] - total[136:144]).astype(BF16).astype(F32) * has_below
        total = jnp.zeros((128, 256), F32)
        for i in range(2 * HR + 1):
            lhs = res[t, pl.ds(i, 128), :].astype(BF16)
            total = total + jnp.dot(lhs, table[t, abs(i - HR)], preferred_element_type=F32)
        img[t, x, y, c] = total.astype(BF16)
        whole = (0, 128)
        g_in[t, "q", 0] = give(t, x, y, c, whole, 0, right(1 - t))
        g_in[t, "q", 1] = give(t, x, y, c, whole, 1, left(1 - t))
        g_in[t, "p", 0, 0] = give(t, x, y, c, whole, 4, right(t))
        g_in[t, "p", 0, 1] = give(t, x, y, c, whole, 5, left(t))
        g_in[t, "s", 0, 0] = give(t, x, y, c, whole, 20, sibling)

    def spread_block(t, dq, slot):
        q = (place[1 - t] + dq) % 4
        bx, by = at_place(t, place[t], q)
        g_in[t, "p", slot, 0] = give(t, bx, by, c, (0, 128), 4 + 4 * slot, right(t))
        g_in[t, "p", slot, 1] = give(t, bx, by, c, (0, 128), 5 + 4 * slot, left(t))
        g_in[t, "s", 0, slot] = give(t, bx, by, c, (0, 128), 20 + slot, sibling)

    for t in range(2):
        g_in[t, "q", 0].wait_recv()
        bx, by = at_place(t, place[t], (place[1 - t] + 3) % 4)
        g_in[t, "q", 2] = give(t, bx, by, c, (0, 64), 2, right(1 - t))
        g_in[t, "q", 1].wait_recv()
        bx2, by2 = at_place(t, place[t], (place[1 - t] + 1) % 4)
        g_in[t, "q", 3] = give(t, bx2, by2, c, (64, 64), 3, left(1 - t))
        spread_block(t, 3, 1)
        spread_block(t, 1, 2)
    for t in range(2):
        g_in[t, "q", 2].wait_recv()
        g_in[t, "q", 3].wait_recv()
        spread_block(t, 2, 3)

    offsets = (0, 3, 1, 2)
    for slot in range(4):
        for t in range(2):
            q = (place[1 - t] + offsets[slot]) % 4
            for side, (dp, start, device) in enumerate(((3, 0, right(t)), (1, 64, left(t)))):
                g_in[t, "p", slot, side].wait_recv()
                bx, by = at_place(t, (place[t] + dp) % 4, q)
                g_in[t, "f", slot, side] = give(t, bx, by, c, (start, 64), 6 + 4 * slot + side, device)
                g_in[t, "s", 1 + side, slot] = give(t, bx, by, c, (0, 128), 24 + 4 * side + slot, sibling)
    for slot in range(4):
        for t in range(2):
            q = (place[1 - t] + offsets[slot]) % 4
            g_in[t, "f", slot, 0].wait_recv()
            g_in[t, "f", slot, 1].wait_recv()
            bx, by = at_place(t, (place[t] + 2) % 4, q)
            g_in[t, "s", 3, slot] = give(t, bx, by, c, (0, 128), 32 + slot, sibling)
    for slot in range(4):
        for t in range(2):
            for column in range(4):
                g_in[t, "s", column, slot].wait_recv()
    for copy in list(a_copies.values()) + m_copies + p_copies + pending:
        copy.wait_send()


def cut_kernel(rows_ref, cols_ref, img, out_ref, wide):
    tilts, boxes = out_ref.shape[:2]
    last = img.shape[1] // 16 - 9
    for t in range(tilts):
        for b in range(boxes):
            wide[t * boxes + b, pl.ds(144, 128), :] = jnp.zeros((128, 256), F32)
    for t in range(tilts):
        for b in range(boxes):
            slot = t * boxes + b
            row, col = rows_ref[b, t], cols_ref[b, t]
            top = jnp.minimum(row // 16, last) * 16
            wide[slot, pl.ds(0, 144), :] = img[t, pl.ds(pl.multiple_of(top, 16), 144), :].astype(F32)
            off = row - top
            rough = wide[slot, pl.ds(pl.multiple_of(off // 8 * 8, 8), 136), :]
            fine = pltpu.roll(rough, 136 - off % 8, 0)[:128]
            out_ref[t, b] = pltpu.roll(fine, 256 - col, 1)[:, :128].astype(BF16)


def exchange_kernel(groups, windows, out_ref, send_sems, recv_sems):
    me, tile = lax.axis_index("tilt"), lax.axis_index("tile")
    for d in range(1, groups):
        signal(((me + d) % groups, tile))
    pl.semaphore_wait(pltpu.get_barrier_semaphore(), groups - 1)
    copies = []
    for k, d in enumerate((4, 3, 5, 2, 6, 1, 7)):
        target = (me + d) % groups
        copy = remote(
            windows.at[:, :, pl.ds(pl.multiple_of(16 * target, 16), 16), :], out_ref.at[me],
            send_sems.at[k], recv_sems.at[k], (target, tile),
        )
        copy.start()
        copies.append(copy)
    out_ref[me] = windows[:, :, pl.ds(pl.multiple_of(16 * me, 16), 16), :]
    for copy in copies:
        copy.wait()


def back_kernel(scale, tap, near, far, rows_ref, out_ref, lines):
    step = pl.program_id(0)

    @pl.when(step == 0)
    def _():
        for t in range(rows_ref.shape[0]):
            lines[t // 2, :, pl.ds(128 * (t % 2), 128)] = rows_ref[t]

    apart = offsets_c_minus_x(True)
    depth = out_ref.shape[1]
    for k in range(depth // 2):
        layer = step * depth + 2 * k

        def add(g, acc):
            tile_w = shear_tile(tap, near, far, 2 * g, layer, apart, True)
            return acc + jnp.dot(lines[g], tile_w, preferred_element_type=F32)

        acc = lax.fori_loop(0, lines.shape[0], add, jnp.zeros((lines.shape[1], 256), F32), unroll=2)
        acc = acc * scale
        out_ref[:, 2 * k, :] = acc[:, :128]
        out_ref[:, 2 * k + 1, :] = acc[:, 128:]


VMEM = pl.BlockSpec(memory_space=pltpu.VMEM)
SMEM = pl.BlockSpec(memory_space=pltpu.SMEM)


def call_project(volumes, tables, groups):
    boxes, slab, depth, width = volumes.shape
    lines = boxes * slab
    return pl.pallas_call(
        functools.partial(project_kernel, groups),
        out_shape=jax.ShapeDtypeStruct((2, boxes, slab * groups, width), BF16),
        in_specs=[SMEM] * 3 + [VMEM],
        out_specs=VMEM,
        scratch_shapes=[
            pltpu.VMEM((lines * depth, width), F32),
            pltpu.VMEM((depth // 2, lines, 2 * width), BF16),
            pltpu.VMEM((groups, 2, boxes, slab, width), BF16),
            pltpu.SemaphoreType.DMA((groups,)),
            pltpu.SemaphoreType.DMA((groups,)),
        ],
        compiler_params=pltpu.CompilerParams(
            collective_id=0, has_side_effects=True, vmem_limit_bytes=32 * MIB
        ),
    )(*tables, volumes.reshape(lines * depth, width))


def call_place(windows, rows, cols, strips):
    return pl.pallas_call(
        place_kernel,
        out_shape=jax.ShapeDtypeStruct((2, strips, 128, 256), BF16),
        in_specs=[SMEM, SMEM, VMEM],
        out_specs=VMEM,
        scratch_shapes=[pltpu.VMEM((2, (strips + 1) * 128 + 128, 256), F32)],
        compiler_params=pltpu.CompilerParams(vmem_limit_bytes=40 * MIB),
    )(rows, cols, windows)


def call_image(canvas, spread, measured):
    dma = lambda *shape: pltpu.SemaphoreType.DMA(shape)
    blocks = lambda *shape: pltpu.VMEM(shape, BF16)
    return pl.pallas_call(
        image_kernel,
        out_shape=(
            jax.ShapeDtypeStruct((2, 128, 256), F32),
            jax.ShapeDtypeStruct((2, 4, 4, 2, 128, 256), BF16),
        ),
        in_specs=[SMEM, VMEM, VMEM],
        out_specs=(VMEM, VMEM),
        scratch_shapes=[
            blocks(2, 4, 4, 128, 256),
            blocks(2, 3, 4, 128, 256),
            blocks(2, 2, 2, 128, 256),
            blocks(2, 2, 4, 128, 256),
            blocks(2, 3, 128, 256),
            blocks(2, 2, 64, 256),
            blocks(2, 2, 128, 256),
            pltpu.VMEM((2, 4, 128, 256), F32),
            blocks(2, 9, 256, 256),
            blocks(2, 128, 256),
            pltpu.VMEM((2, 160, 256), F32),
            blocks(2, 2, 16, 256),
            pltpu.VMEM((2, 2, 8, 256), F32),
            pltpu.VMEM((2, 144, 256), F32),
            dma(2, 2, 4),
            dma(2, 2, 6),
            dma(2, 2, 6),
            dma(2, 4),
            dma(2, 2, 36),
        ],
        compiler_params=pltpu.CompilerParams(
            collective_id=1, has_side_effects=True, vmem_limit_bytes=48 * MIB
        ),
    )(spread, canvas.reshape(2, 4, 4, 2, 128, 256), measured)


def call_cut(image, rows, cols):
    boxes, tilts = rows.shape
    return pl.pallas_call(
        cut_kernel,
        out_shape=jax.ShapeDtypeStruct((tilts, boxes, 128, 128), BF16),
        in_specs=[SMEM, SMEM, VMEM],
        out_specs=VMEM,
        scratch_shapes=[pltpu.VMEM((tilts * boxes, 272, 256), F32)],
        compiler_params=pltpu.CompilerParams(vmem_limit_bytes=32 * MIB),
    )(rows, cols, image.reshape(2, 4096, 256))


def call_exchange(windows, groups):
    tilts, boxes = windows.shape[:2]
    return pl.pallas_call(
        functools.partial(exchange_kernel, groups),
        out_shape=jax.ShapeDtypeStruct((groups, tilts, boxes, 16, 128), BF16),
        in_specs=[VMEM],
        out_specs=VMEM,
        scratch_shapes=[pltpu.SemaphoreType.DMA((7,)), pltpu.SemaphoreType.DMA((7,))],
        compiler_params=pltpu.CompilerParams(
            collective_id=2, has_side_effects=True, vmem_limit_bytes=32 * MIB
        ),
    )(windows)


def call_back(back_rows, tables, shape):
    boxes, slab, depth, width = shape
    lines = boxes * slab
    tilts = back_rows.shape[0] * 2
    per_step = 8
    return pl.pallas_call(
        functools.partial(back_kernel, 1.0 / tilts),
        grid=(depth // per_step,),
        out_shape=jax.ShapeDtypeStruct((lines, depth, width), F32),
        in_specs=[SMEM] * 3 + [pl.BlockSpec((tilts, lines, width), lambda i: (0, 0, 0))],
        out_specs=pl.BlockSpec((lines, per_step, width), lambda i: (0, i, 0)),
        scratch_shapes=[pltpu.VMEM((tilts // 2, lines, 2 * width), BF16)],
        compiler_params=pltpu.CompilerParams(vmem_limit_bytes=32 * MIB),
    )(*tables, back_rows.reshape(tilts, lines, width)).reshape(shape)


def shear_tables(angles, depth):
    layers = jnp.arange(depth, dtype=F32)
    shift = (layers - (depth - 1) / 2.0) * jnp.sin(angles)[:, None]
    tap = jnp.floor(shift)
    weight = lambda offset: jnp.maximum(0.0, 1.0 - jnp.abs(offset - shift)).astype(BF16).astype(F32)
    return tap, weight(tap), weight(tap + 1.0)


def spread_table(defocus):
    steps = jnp.arange(HR + 1, dtype=F32)
    rho_sq = (steps[:, None] ** 2 + steps[None, :] ** 2).reshape(1, -1)
    scale = float(HR * HR)
    values = jnp.exp(-rho_sq / (2.0 * scale)) * jnp.cos(defocus[:, None] * rho_sq) / scale
    return values.astype(BF16).astype(F32)


def shards(volumes, angles, defocus, row_offsets, col_offsets, measured):
    groups = lax.axis_size("tilt")
    tables = shear_tables(angles, volumes.shape[2])
    windows = call_project(volumes, tables, groups)
    canvas = call_place(windows, row_offsets, col_offsets, lax.axis_size("tile"))
    residual, image = call_image(canvas, spread_table(defocus), measured)
    back_rows = call_exchange(call_cut(image, row_offsets, col_offsets), groups)
    return residual, call_back(back_rows, tables, volumes.shape)


def solution(mesh):
    in_specs = (
        P("tile", "tilt", None, None),
        P(),
        P("tilt"),
        P("tile", "tilt"),
        P("tile", "tilt"),
        P("tilt", "tile", None),
    )
    out_specs = (P("tilt", "tile", None), P("tile", "tilt", None, None))
    return jax.shard_map(shards, mesh=mesh, in_specs=in_specs, out_specs=out_specs, check_vma=False)
```

```python
import functools

import jax
import jax.numpy as jnp
from jax import lax
from jax.experimental import pallas as pl
from jax.experimental.pallas import tpu as pltpu
from jax.sharding import PartitionSpec as P

HR = 8
MESH = pl.DeviceIdType.MESH
BF16 = jnp.bfloat16
F32 = jnp.float32
MIB = 1 << 20


def signal(device):
    pl.semaphore_signal(
        pltpu.get_barrier_semaphore(), inc=1, device_id=device, device_id_type=MESH
    )


def remote(src, dst, send_sem, recv_sem, device):
    return pltpu.make_async_remote_copy(
        src_ref=src, dst_ref=dst, send_sem=send_sem, recv_sem=recv_sem,
        device_id=device, device_id_type=MESH,
    )


def offsets_c_minus_x(transposed):
    rows = lax.broadcasted_iota(jnp.int32, (128, 128), 0)
    cols = lax.broadcasted_iota(jnp.int32, (128, 128), 1)
    return ((rows - cols) if transposed else (cols - rows)).astype(F32).astype(BF16)


def sine(x):
    square = x * x
    value = -1.0 / 39916800.0 + square * (1.0 / 6227020800.0)
    for factor in (1.0 / 362880.0, -1.0 / 5040.0, 1.0 / 120.0, -1.0 / 6.0):
        value = factor + square * value
    return x + x * (square * value)


def sines_into(angles, sines):
    for t in range(angles.shape[0]):
        sines[t] = sine(angles[t])


def shear_block(sines, tilt, layer, apart):
    shift = (jnp.asarray(layer, jnp.int32).astype(F32) - 31.5) * sines[tilt]
    tap = shift.astype(jnp.int32).astype(F32)
    tap = jnp.where(tap > shift, tap - 1.0, tap)
    all_of = lambda value: jnp.full((128, 128), value, F32).astype(BF16)
    near = jnp.maximum(0.0, 1.0 - jnp.abs(tap - shift))
    far = jnp.maximum(0.0, 1.0 - jnp.abs(tap + 1.0 - shift))
    zero = jnp.zeros((128, 128), BF16)
    return jnp.where(apart == all_of(tap), all_of(near), jnp.where(apart == all_of(tap + 1.0), all_of(far), zero))


def shear_tile(sines, tilt, layer, apart, transposed):
    make = lambda t, z: shear_block(sines, tilt + t, layer + z, apart)
    if transposed:
        parts = [[make(t, z) for z in range(2)] for t in range(2)]
    else:
        parts = [[make(t, z) for t in range(2)] for z in range(2)]
    return jnp.concatenate([jnp.concatenate(row, axis=1) for row in parts], axis=0)


def flip_matrix():
    rows = lax.broadcasted_iota(jnp.int32, (128, 128), 0)
    cols = lax.broadcasted_iota(jnp.int32, (128, 128), 1)
    return jnp.where(rows + cols == 127, 1.0, 0.0).astype(BF16)


def flipped(x, flip):
    high = x.astype(BF16)
    low = (x - high.astype(F32)).astype(BF16)
    return jnp.dot(
        jnp.concatenate([high, low], axis=1), jnp.concatenate([flip, flip], axis=0), preferred_element_type=F32
    )


def project_kernel(groups, angles, v_ref, out_ref, sines, wide, pairs, sent, send_sems, recv_sems):
    me, tile = lax.axis_index("tilt"), lax.axis_index("tile")
    for d in range(1, groups):
        signal(((me + d) % groups, tile))
    sines_into(angles, sines)
    rows = v_ref.shape[0]
    lines = rows // 64

    def widen(i, carry):
        at = pl.ds(pl.multiple_of(i * 512, 512), 512)
        wide[at, :] = v_ref[at, :].astype(F32)
        return carry

    lax.fori_loop(0, rows // 512, widen, 0)
    flip = flip_matrix()

    def gather(k, carry):
        layer = lambda z: wide[pl.ds(z, lines, stride=64), :]
        top = jnp.concatenate([layer(2 * k), layer(2 * k + 1)], axis=1).astype(BF16)
        mirror = jnp.concatenate([layer(63 - 2 * k), layer(62 - 2 * k)], axis=0).astype(BF16)
        mirror = jnp.dot(mirror, flip, preferred_element_type=F32).astype(BF16)
        pairs[k] = jnp.concatenate([top, jnp.concatenate([mirror[:lines], mirror[lines:]], axis=1)], axis=0)
        return carry

    lax.fori_loop(0, 16, gather, 0)
    pl.semaphore_wait(pltpu.get_barrier_semaphore(), groups - 1)
    apart = offsets_c_minus_x(False)
    mine = pl.ds(pl.multiple_of(16 * me, 16), 16)

    def windows_of(target):
        acc = jnp.zeros((2 * lines, 256), F32)
        for k in range(16):
            acc = acc + jnp.dot(
                pairs[k], shear_tile(sines, 2 * target, 2 * k, apart, False), preferred_element_type=F32
            )
        mirror = flipped(jnp.concatenate([acc[lines:, :128], acc[lines:, 128:]], axis=0), flip)
        both = (acc[:lines, :128] + mirror[:lines], acc[:lines, 128:] + mirror[lines:])
        return [half.astype(BF16).reshape(lines // 16, 16, 128) for half in both]

    def copy_of(step):
        d = jnp.where(step % 2 == 0, 4 + step // 2, 4 - (step + 1) // 2)
        target = (me + d) % groups
        return target, remote(
            sent.at[step], out_ref.at[:, :, mine, :], send_sems.at[step], recv_sems.at[step], (target, tile)
        )

    def project(step, carry):
        target, copy = copy_of(step)
        both = windows_of(target)
        for t in range(2):
            sent[step, t] = both[t]
        copy.start()
        return carry

    lax.fori_loop(0, groups - 1, project, 0)
    both = windows_of(me)
    for t in range(2):
        out_ref[t, :, mine, :] = both[t]

    def finish(step, carry):
        copy_of(step)[1].wait()
        return carry

    lax.fori_loop(0, groups - 1, finish, 0)


def place_kernel(rows_ref, cols_ref, w_ref, out_ref, canvas):
    tilts, boxes = w_ref.shape[:2]
    strips = out_ref.shape[1]

    def clear(i, carry):
        at = pl.ds(pl.multiple_of(i * 136, 8), 136)
        for t in range(tilts):
            canvas[t, at, :] = jnp.zeros((136, 256), F32)
        return carry

    lax.fori_loop(0, canvas.shape[1] // 136, clear, 0)
    for b in range(boxes):
        for t in range(tilts):
            row, col = rows_ref[t, b], cols_ref[t, b]
            window = jnp.concatenate([w_ref[t, b].astype(F32), jnp.zeros((128, 128), F32)], axis=1)
            window = pltpu.roll(window, col, 1)
            window = jnp.concatenate([window, jnp.zeros((8, 256), F32)], axis=0)
            window = pltpu.roll(window, row % 8, 0)
            at = pl.ds(pl.multiple_of(row // 8 * 8, 8), 136)
            canvas[t, at, :] = canvas[t, at, :] + window

    def narrow(i, carry):
        at = pl.ds(pl.multiple_of(i * 128, 128), 128)
        for t in range(tilts):
            out_ref[t, i] = canvas[t, at, :].astype(BF16)
        return carry

    lax.fori_loop(0, strips, narrow, 0)


def image_kernel(
    defocus, can, measured, residual, img, spread_wide, spread,
    r_a, s_b, o_b, f_b, s_c, o_c, f_c, own, table, pred_half, pred, halo, m_halo, res,
    a_sems, b_sems, c_sems, h_sems, g_sems,
):
    z, tile = lax.axis_index("tilt"), lax.axis_index("tile")
    x, y, c = tile // 8, (tile // 2) % 4, tile % 2
    other = 1 - c

    def dev(dx, dy):
        return (z, ((x + dx) % 4) * 8 + ((y + dy) % 4) * 2 + c)

    sibling = (z, x * 8 + y * 2 + other)
    below, above = (z, (tile + 1) % 32), (z, (tile + 31) % 32)
    right = lambda axis: dev(1, 0) if axis == 0 else dev(0, 1)
    left = lambda axis: dev(3, 0) if axis == 0 else dev(0, 3)
    place = (x, y)
    for device in (sibling, below, above, right(0), left(0), right(1), left(1)):
        signal(device)
    pl.semaphore_wait(pltpu.get_barrier_semaphore(), 7)

    steps = (2, 1, 3, 0)

    def block(ref, t, p, core):
        return ref.at[0, p, :, core] if t == 0 else ref.at[1, :, p, core]

    a_copies = {}
    for k, d in enumerate(steps):
        for t in range(2):
            p = (place[t] + d) % 4
            copy = remote(
                block(can, t, p, other), r_a.at[t, k], a_sems.at[0, t, k], a_sems.at[1, t, k], sibling
            )
            copy.start()
            a_copies[t, k] = copy
    m_copies = []
    for k, (device, start) in enumerate(((below, 120), (above, 0))):
        copy = remote(
            measured.at[:, pl.ds(start, 8), :], m_halo.at[k], h_sems.at[0, k], h_sems.at[1, k], device
        )
        copy.start()
        m_copies.append(copy)

    down = lax.broadcasted_iota(jnp.int32, (16, 128), 0).astype(F32)
    along = lax.broadcasted_iota(jnp.int32, (16, 128), 1).astype(F32)
    rho_sq = down * down + along * along
    scale = float(HR * HR)
    for t in range(2):
        spread_wide[t] = jnp.exp(-rho_sq / (2.0 * scale)) * jnp.cos(defocus[t] * rho_sq) / scale
    to_scalars = pltpu.make_async_copy(spread_wide, spread, h_sems.at[0, 4])
    to_scalars.start()
    to_scalars.wait()

    def fill(i, carry):
        lanes = lax.broadcasted_iota(jnp.int32, (16, 256), 1)
        subs = lax.broadcasted_iota(jnp.int32, (16, 256), 0) + i * 16
        apart = jnp.abs(lanes - subs).astype(F32).astype(BF16)
        masks = [apart == jnp.full((16, 256), j, F32).astype(BF16) for j in range(HR + 1)]
        for t in range(2):
            for a in range(HR + 1):
                value = jnp.zeros((16, 256), BF16)
                for j in range(HR + 1):
                    value = jnp.where(masks[j], jnp.full((16, 256), spread[t, a, j], F32).astype(BF16), value)
                table[t, a, pl.ds(pl.multiple_of(i * 16, 16), 16), :] = value
        return carry

    lax.fori_loop(0, 16, fill, 0)

    pending = []

    def go(src, dst, sems, t, k, device):
        copy = remote(src, dst, sems.at[0, t, k], sems.at[1, t, k], device)
        copy.start()
        pending.append(copy)
        return copy

    def local_b(t, k, half):
        d = steps[k]
        p = (place[t] + d) % 4
        at = pl.ds(2 * half, 2)
        mine = can[0, p, at, c] if t == 0 else can[1, at, p, c]
        return mine.astype(F32) + r_a[t, k, at].astype(F32)

    b_in = {}
    for t in range(2):
        a_copies[t, 0].wait_recv()
        for h, device in ((0, right(t)), (1, left(t))):
            s_b[t, 0, pl.ds(2 * h, 2)] = local_b(t, 0, h).astype(BF16)
            b_in[t, "opp", h] = go(s_b.at[t, 0, pl.ds(2 * h, 2)], o_b.at[t, h], b_sems, t, h, device)
    for t in range(2):
        for k, h, device in ((1, 1, right(t)), (2, 0, left(t))):
            a_copies[t, k].wait_recv()
            at = pl.ds(2 * h, 2)
            s_b[t, k, at] = local_b(t, k, h).astype(BF16)
            b_in[t, "free", k] = go(s_b.at[t, k, at], f_b.at[t, k - 1, at], b_sems, t, 1 + k, device)
    for t in range(2):
        for k, h, device in ((1, 0, right(t)), (2, 1, left(t))):
            at = pl.ds(2 * h, 2)
            b_in[t, "opp", h].wait_recv()
            s_b[t, k, at] = (local_b(t, k, h) + o_b[t, h].astype(F32)).astype(BF16)
            b_in[t, "bound", k] = go(s_b.at[t, k, at], f_b.at[t, k - 1, at], b_sems, t, 3 + k, device)
    for t in range(2):
        a_copies[t, 3].wait_recv()
        for h in range(2):
            own[t, pl.ds(2 * h, 2)] = local_b(t, 3, h)
        for k in (1, 2):
            b_in[t, "free", k].wait_recv()
            b_in[t, "bound", k].wait_recv()

    def local_c(t, k, half):
        q = (place[1 - t] + steps[k]) % 4
        at = pl.ds(64 * half, 64)
        return own[t, q, at, :] + f_b[t, 0, q, at, :].astype(F32) + f_b[t, 1, q, at, :].astype(F32)

    c_in = {}
    for t in range(2):
        for h, device in ((0, right(1 - t)), (1, left(1 - t))):
            at = pl.ds(64 * h, 64)
            s_c[t, 0, at] = local_c(t, 0, h).astype(BF16)
            c_in[t, "opp", h] = go(s_c.at[t, 0, at], o_c.at[t, h], c_sems, t, h, device)
        for k, h, device in ((1, 1, right(1 - t)), (2, 0, left(1 - t))):
            at = pl.ds(64 * h, 64)
            s_c[t, k, at] = local_c(t, k, h).astype(BF16)
            c_in[t, "free", k] = go(s_c.at[t, k, at], f_c.at[t, k - 1, at], c_sems, t, 1 + k, device)
    for t in range(2):
        for k, h, device in ((1, 0, right(1 - t)), (2, 1, left(1 - t))):
            at = pl.ds(64 * h, 64)
            c_in[t, "opp", h].wait_recv()
            s_c[t, k, at] = (local_c(t, k, h) + o_c[t, h].astype(F32)).astype(BF16)
            c_in[t, "bound", k] = go(s_c.at[t, k, at], f_c.at[t, k - 1, at], c_sems, t, 3 + k, device)
    for t in range(2):
        for k in (1, 2):
            c_in[t, "free", k].wait_recv()
            c_in[t, "bound", k].wait_recv()
        total = jnp.concatenate([local_c(t, 3, h) for h in range(2)], axis=0)
        total = total + f_c[t, 0].astype(F32) + f_c[t, 1].astype(F32)
        pred_half[t] = total.astype(BF16)
        pred[t, pl.ds(16, 128), :] = pred_half[t].astype(F32)

    p_copies = []
    for k, (device, start) in enumerate(((below, 112), (above, 0))):
        copy = remote(
            pred_half.at[:, pl.ds(start, 16), :], halo.at[k], h_sems.at[0, 2 + k], h_sems.at[1, 2 + k], device
        )
        copy.start()
        p_copies.append(copy)
    has_above = jnp.where(tile > 0, 1.0, 0.0).astype(F32)
    has_below = jnp.where(tile < 31, 1.0, 0.0).astype(F32)
    for copy in m_copies + p_copies:
        copy.wait_recv()
    for t in range(2):
        pred[t, pl.ds(0, 16), :] = halo[0, t].astype(F32) * has_above
        pred[t, pl.ds(144, 16), :] = halo[1, t].astype(F32) * has_below

    g_in = {}

    def give(t, bx, by, core, rows, k, device):
        at = pl.ds(rows[0], rows[1])
        where = img.at[t, bx, by, core, at]
        copy = remote(where, where, g_sems.at[0, t, k], g_sems.at[1, t, k], device)
        copy.start()
        pending.append(copy)
        return copy

    def at_place(t, p, q):
        return (p, q) if t == 0 else (q, p)

    for t in range(2):
        total = jnp.zeros((144, 256), F32)
        for i in range(2 * HR + 1):
            lhs = pred[t, pl.ds(i, 144), :].astype(BF16)
            total = total + jnp.dot(lhs, table[t, abs(i - HR)], preferred_element_type=F32)
        inner = measured[t] - total[8:136]
        residual[t] = inner
        res[t, pl.ds(8, 128), :] = inner.astype(BF16).astype(F32)
        res[t, pl.ds(0, 8), :] = (m_halo[0, t] - total[0:8]).astype(BF16).astype(F32) * has_above
        res[t, pl.ds(136, 8), :] = (m_halo[1, t] - total[136:144]).astype(BF16).astype(F32) * has_below
        total = jnp.zeros((128, 256), F32)
        for i in range(2 * HR + 1):
            lhs = res[t, pl.ds(i, 128), :].astype(BF16)
            total = total + jnp.dot(lhs, table[t, abs(i - HR)], preferred_element_type=F32)
        img[t, x, y, c] = total.astype(BF16)
        whole = (0, 128)
        g_in[t, "q", 0] = give(t, x, y, c, whole, 0, right(1 - t))
        g_in[t, "q", 1] = give(t, x, y, c, whole, 1, left(1 - t))
        g_in[t, "p", 0, 0] = give(t, x, y, c, whole, 4, right(t))
        g_in[t, "p", 0, 1] = give(t, x, y, c, whole, 5, left(t))
        g_in[t, "s", 0, 0] = give(t, x, y, c, whole, 20, sibling)

    def spread_block(t, dq, slot):
        q = (place[1 - t] + dq) % 4
        bx, by = at_place(t, place[t], q)
        g_in[t, "p", slot, 0] = give(t, bx, by, c, (0, 128), 4 + 4 * slot, right(t))
        g_in[t, "p", slot, 1] = give(t, bx, by, c, (0, 128), 5 + 4 * slot, left(t))
        g_in[t, "s", 0, slot] = give(t, bx, by, c, (0, 128), 20 + slot, sibling)

    for t in range(2):
        g_in[t, "q", 0].wait_recv()
        bx, by = at_place(t, place[t], (place[1 - t] + 3) % 4)
        g_in[t, "q", 2] = give(t, bx, by, c, (0, 64), 2, right(1 - t))
        g_in[t, "q", 1].wait_recv()
        bx2, by2 = at_place(t, place[t], (place[1 - t] + 1) % 4)
        g_in[t, "q", 3] = give(t, bx2, by2, c, (64, 64), 3, left(1 - t))
        spread_block(t, 3, 1)
        spread_block(t, 1, 2)
    for t in range(2):
        g_in[t, "q", 2].wait_recv()
        g_in[t, "q", 3].wait_recv()
        spread_block(t, 2, 3)

    offsets = (0, 3, 1, 2)
    for slot in range(4):
        for t in range(2):
            q = (place[1 - t] + offsets[slot]) % 4
            for side, (dp, start, device) in enumerate(((3, 0, right(t)), (1, 64, left(t)))):
                g_in[t, "p", slot, side].wait_recv()
                bx, by = at_place(t, (place[t] + dp) % 4, q)
                g_in[t, "f", slot, side] = give(t, bx, by, c, (start, 64), 6 + 4 * slot + side, device)
                g_in[t, "s", 1 + side, slot] = give(t, bx, by, c, (0, 128), 24 + 4 * side + slot, sibling)
    for slot in range(4):
        for t in range(2):
            q = (place[1 - t] + offsets[slot]) % 4
            g_in[t, "f", slot, 0].wait_recv()
            g_in[t, "f", slot, 1].wait_recv()
            bx, by = at_place(t, (place[t] + 2) % 4, q)
            g_in[t, "s", 3, slot] = give(t, bx, by, c, (0, 128), 32 + slot, sibling)
    for slot in range(4):
        for t in range(2):
            for column in range(4):
                g_in[t, "s", column, slot].wait_recv()
    for copy in list(a_copies.values()) + m_copies + p_copies + pending:
        copy.wait_send()


def cut_kernel(rows_ref, cols_ref, img, out_ref, wide):
    tilts, boxes = out_ref.shape[:2]
    last = img.shape[1] // 16 - 9
    for t in range(tilts):
        for b in range(boxes):
            wide[t * boxes + b, pl.ds(144, 128), :] = jnp.zeros((128, 256), F32)
    for t in range(tilts):
        for b in range(boxes):
            slot = t * boxes + b
            row, col = rows_ref[t, b], cols_ref[t, b]
            top = jnp.minimum(row // 16, last) * 16
            wide[slot, pl.ds(0, 144), :] = img[t, pl.ds(pl.multiple_of(top, 16), 144), :].astype(F32)
            off = row - top
            rough = wide[slot, pl.ds(pl.multiple_of(off // 8 * 8, 8), 136), :]
            fine = pltpu.roll(rough, 136 - off % 8, 0)[:128]
            out_ref[t, b] = pltpu.roll(fine, 256 - col, 1)[:, :128].astype(BF16)


def back_kernel(groups, scale, angles, windows, out_ref, sines, got, lines, sums, blocks, send_sems, recv_sems, sems):
    me, tile = lax.axis_index("tilt"), lax.axis_index("tile")
    for d in range(1, groups):
        signal(((me + d) % groups, tile))
    sines_into(angles, sines)
    flip = flip_matrix()
    count = lines.shape[1] // 2
    pl.semaphore_wait(pltpu.get_barrier_semaphore(), groups - 1)
    copies = {}
    for d in (1, 7, 2, 6, 3, 5, 4):
        target = (me + d) % groups
        copies[d] = remote(
            windows.at[:, :, pl.ds(pl.multiple_of(16 * target, 16), 16), :], got.at[d],
            send_sems.at[d], recv_sems.at[d], (target, tile),
        )
        copies[d].start()
    apart = offsets_c_minus_x(True)

    def take(slot, rows):
        for t in range(2):
            at = pl.ds(128 * t, 128)
            line = rows[t].reshape(count, 128)
            lines[slot, pl.ds(0, count), at] = line
            lines[slot, pl.ds(count, count), at] = jnp.dot(line, flip, preferred_element_type=F32).astype(BF16)

    def copies_of(i):
        low = pltpu.make_async_copy(
            blocks.at[0, i], out_ref.at[:, pl.ds(pl.multiple_of(8 * i, 8), 8), :], sems.at[0, i]
        )
        high = pltpu.make_async_copy(
            blocks.at[1, i], out_ref.at[:, pl.ds(pl.multiple_of(56 - 8 * i, 8), 8), :], sems.at[1, i]
        )
        return low, high

    order = ((0, 1), (7, 2), (6, 3), (5, 4))
    for stage, pair in enumerate(order):
        for slot, d in enumerate(pair):
            if d == 0:
                take(slot, windows[:, :, pl.ds(pl.multiple_of(16 * me, 16), 16), :])
            else:
                copies[d].wait_recv()
                take(slot, got[d])
        from_group = [(me - d + groups) % groups for d in pair]

        def product(i, k):
            acc = jnp.zeros((2 * count, 256), F32)
            for slot in range(2):
                weights = shear_tile(sines, 2 * from_group[slot], 8 * i + 2 * k, apart, True)
                acc = acc + jnp.dot(lines[slot], weights, preferred_element_type=F32)
            return acc

        def first(i, carry):
            for k in range(4):
                sums[4 * i + k] = product(i, k)
            return carry

        def middle(i, carry):
            for k in range(4):
                sums[4 * i + k] = sums[4 * i + k] + product(i, k)
            return carry

        def last(i, carry):
            for k in range(4):
                acc = (sums[4 * i + k] + product(i, k)) * scale
                blocks[0, i, :, 2 * k, :] = acc[:count, :128]
                blocks[0, i, :, 2 * k + 1, :] = acc[:count, 128:]
                mirror = flipped(jnp.concatenate([acc[count:, :128], acc[count:, 128:]], axis=0), flip)
                blocks[1, i, :, 7 - 2 * k, :] = mirror[:count]
                blocks[1, i, :, 6 - 2 * k, :] = mirror[count:]
            for copy in copies_of(i):
                copy.start()
            return carry

        lax.fori_loop(0, 4, first if stage == 0 else last if stage == 3 else middle, 0)

    def finish(i, carry):
        for copy in copies_of(i):
            copy.wait()
        return carry

    lax.fori_loop(0, 4, finish, 0)
    for copy in copies.values():
        copy.wait_send()


VMEM = pl.BlockSpec(memory_space=pltpu.VMEM)
SMEM = pl.BlockSpec(memory_space=pltpu.SMEM)


def call_project(volumes, angles, groups):
    boxes, slab, depth, width = volumes.shape
    lines = boxes * slab
    return pl.pallas_call(
        functools.partial(project_kernel, groups),
        out_shape=jax.ShapeDtypeStruct((2, boxes, slab * groups, width), BF16),
        in_specs=[SMEM, VMEM],
        out_specs=VMEM,
        scratch_shapes=[
            pltpu.SMEM(angles.shape, F32),
            pltpu.VMEM((lines * depth, width), F32),
            pltpu.VMEM((depth // 4, 2 * lines, 2 * width), BF16),
            pltpu.VMEM((groups, 2, boxes, slab, width), BF16),
            pltpu.SemaphoreType.DMA((groups,)),
            pltpu.SemaphoreType.DMA((groups,)),
        ],
        compiler_params=pltpu.CompilerParams(
            collective_id=0, has_side_effects=True, vmem_limit_bytes=20 * MIB
        ),
    )(angles, volumes.reshape(lines * depth, width))


def call_place(windows, rows, cols, strips):
    return pl.pallas_call(
        place_kernel,
        out_shape=jax.ShapeDtypeStruct((2, strips, 128, 256), BF16),
        in_specs=[SMEM, SMEM, VMEM],
        out_specs=VMEM,
        scratch_shapes=[pltpu.VMEM((2, (strips + 1) * 128 + 128, 256), F32)],
        compiler_params=pltpu.CompilerParams(vmem_limit_bytes=20 * MIB),
    )(rows, cols, windows)


def call_image(canvas, defocus, measured):
    dma = lambda *shape: pltpu.SemaphoreType.DMA(shape)
    blocks = lambda *shape: pltpu.VMEM(shape, BF16)
    return pl.pallas_call(
        image_kernel,
        out_shape=(
            jax.ShapeDtypeStruct((2, 128, 256), F32),
            jax.ShapeDtypeStruct((2, 4, 4, 2, 128, 256), BF16),
        ),
        in_specs=[SMEM, VMEM, VMEM],
        out_specs=(VMEM, VMEM),
        scratch_shapes=[
            pltpu.VMEM((2, 16, 128), F32),
            pltpu.SMEM((2, 16, 128), F32),
            blocks(2, 4, 4, 128, 256),
            blocks(2, 3, 4, 128, 256),
            blocks(2, 2, 2, 128, 256),
            blocks(2, 2, 4, 128, 256),
            blocks(2, 3, 128, 256),
            blocks(2, 2, 64, 256),
            blocks(2, 2, 128, 256),
            pltpu.VMEM((2, 4, 128, 256), F32),
            blocks(2, 9, 256, 256),
            blocks(2, 128, 256),
            pltpu.VMEM((2, 160, 256), F32),
            blocks(2, 2, 16, 256),
            pltpu.VMEM((2, 2, 8, 256), F32),
            pltpu.VMEM((2, 144, 256), F32),
            dma(2, 2, 4),
            dma(2, 2, 6),
            dma(2, 2, 6),
            dma(2, 5),
            dma(2, 2, 36),
        ],
        compiler_params=pltpu.CompilerParams(
            collective_id=1, has_side_effects=True, vmem_limit_bytes=24 * MIB
        ),
    )(defocus, canvas.reshape(2, 4, 4, 2, 128, 256), measured)


def call_cut(image, rows, cols):
    tilts, boxes = rows.shape
    return pl.pallas_call(
        cut_kernel,
        out_shape=jax.ShapeDtypeStruct((tilts, boxes, 128, 128), BF16),
        in_specs=[SMEM, SMEM, VMEM],
        out_specs=VMEM,
        scratch_shapes=[pltpu.VMEM((tilts * boxes, 272, 256), F32)],
        compiler_params=pltpu.CompilerParams(vmem_limit_bytes=16 * MIB),
    )(rows, cols, image.reshape(2, 4096, 256))


def call_back(windows, angles, shape, groups):
    boxes, slab, depth, width = shape
    lines = boxes * slab
    return pl.pallas_call(
        functools.partial(back_kernel, groups, 1.0 / (2 * groups)),
        out_shape=jax.ShapeDtypeStruct((lines, depth, width), F32),
        in_specs=[SMEM, VMEM],
        out_specs=pl.BlockSpec(memory_space=pl.ANY),
        scratch_shapes=[
            pltpu.SMEM(angles.shape, F32),
            pltpu.VMEM((groups, 2, boxes, slab, width), BF16),
            pltpu.VMEM((2, 2 * lines, 2 * width), BF16),
            pltpu.VMEM((16, 2 * lines, 2 * width), F32),
            pltpu.VMEM((2, 4, lines, 8, width), F32),
            pltpu.SemaphoreType.DMA((groups,)),
            pltpu.SemaphoreType.DMA((groups,)),
            pltpu.SemaphoreType.DMA((2, 4)),
        ],
        compiler_params=pltpu.CompilerParams(
            collective_id=2, has_side_effects=True, vmem_limit_bytes=20 * MIB
        ),
    )(angles, windows).reshape(shape)


def shards(volumes, angles, defocus, row_offsets, col_offsets, measured):
    groups = lax.axis_size("tilt")
    windows = call_project(volumes, angles, groups)
    rows, cols = row_offsets.T, col_offsets.T
    canvas = call_place(windows, rows, cols, lax.axis_size("tile"))
    residual, image = call_image(canvas, defocus, measured)
    back_windows = call_cut(image, rows, cols)
    return residual, call_back(back_windows, angles, volumes.shape, groups)


def solution(mesh):
    in_specs = (
        P("tile", "tilt", None, None),
        P(),
        P("tilt"),
        P("tile", "tilt"),
        P("tile", "tilt"),
        P("tilt", "tile", None),
    )
    out_specs = (P("tilt", "tile", None), P("tile", "tilt", None, None))
    return jax.shard_map(shards, mesh=mesh, in_specs=in_specs, out_specs=out_specs, check_vma=False)
```

```python
import functools

import jax
import jax.numpy as jnp
from jax import lax
from jax.experimental import pallas as pl
from jax.experimental.pallas import tpu as pltpu
from jax.sharding import PartitionSpec as P

HR = 8
MESH = pl.DeviceIdType.MESH
BF16 = jnp.bfloat16
F32 = jnp.float32
MIB = 1 << 20


def signal(device):
    pl.semaphore_signal(
        pltpu.get_barrier_semaphore(), inc=1, device_id=device, device_id_type=MESH
    )


def remote(src, dst, send_sem, recv_sem, device):
    return pltpu.make_async_remote_copy(
        src_ref=src, dst_ref=dst, send_sem=send_sem, recv_sem=recv_sem,
        device_id=device, device_id_type=MESH,
    )


def offsets_c_minus_x(transposed):
    rows = lax.broadcasted_iota(jnp.int32, (128, 128), 0)
    cols = lax.broadcasted_iota(jnp.int32, (128, 128), 1)
    return ((rows - cols) if transposed else (cols - rows)).astype(F32).astype(BF16)


def sine(x):
    square = x * x
    value = -1.0 / 39916800.0 + square * (1.0 / 6227020800.0)
    for factor in (1.0 / 362880.0, -1.0 / 5040.0, 1.0 / 120.0, -1.0 / 6.0):
        value = factor + square * value
    return x + x * (square * value)


def shear_block(sines, tilt, layer, apart):
    shift = (jnp.asarray(layer, jnp.int32).astype(F32) - 31.5) * sines[tilt]
    tap = shift.astype(jnp.int32).astype(F32)
    tap = jnp.where(tap > shift, tap - 1.0, tap)
    all_of = lambda value: jnp.full((128, 128), value, F32).astype(BF16)
    near = jnp.maximum(0.0, 1.0 - jnp.abs(tap - shift))
    far = jnp.maximum(0.0, 1.0 - jnp.abs(tap + 1.0 - shift))
    zero = jnp.zeros((128, 128), BF16)
    return jnp.where(apart == all_of(tap), all_of(near), jnp.where(apart == all_of(tap + 1.0), all_of(far), zero))


def shear_tile(sines, tilt, layer, apart, transposed):
    make = lambda t, z: shear_block(sines, tilt + t, layer + z, apart)
    if transposed:
        parts = [[make(t, z) for z in range(2)] for t in range(2)]
    else:
        parts = [[make(t, z) for t in range(2)] for z in range(2)]
    return jnp.concatenate([jnp.concatenate(row, axis=1) for row in parts], axis=0)


def flip_matrix():
    rows = lax.broadcasted_iota(jnp.int32, (128, 128), 0)
    cols = lax.broadcasted_iota(jnp.int32, (128, 128), 1)
    return jnp.where(rows + cols == 127, 1.0, 0.0).astype(BF16)


def flipped(x, flip):
    high = x.astype(BF16)
    low = (x - high.astype(F32)).astype(BF16)
    return jnp.dot(
        jnp.concatenate([high, low], axis=1), jnp.concatenate([flip, flip], axis=0), preferred_element_type=F32
    )


def project_part(
    groups, me, tile, sibling, loads, ready, sines, v_ref, out_ref, pair_ref,
    wide, pairs, sent, send_sems, recv_sems, pair_sems,
):
    rows = v_ref.shape[0]
    lines = rows // 64
    parts = len(loads)
    size = rows // parts

    def widen(i, carry):
        at = pl.ds(pl.multiple_of(i * 512, 512), 512)
        wide[at, :] = v_ref[at, :].astype(F32)
        return carry

    for i in range(parts):
        loads[i].wait()
        lax.fori_loop(i * size // 512, (i + 1) * size // 512, widen, 0)
    flip = flip_matrix()

    def gather(k, carry):
        layer = lambda z: wide[pl.ds(z, lines, stride=64), :]
        top = jnp.concatenate([layer(2 * k), layer(2 * k + 1)], axis=1).astype(BF16)
        mirror = jnp.concatenate([layer(63 - 2 * k), layer(62 - 2 * k)], axis=0).astype(BF16)
        mirror = jnp.dot(mirror, flip, preferred_element_type=F32).astype(BF16)
        pairs[k] = jnp.concatenate([top, jnp.concatenate([mirror[:lines], mirror[lines:]], axis=1)], axis=0)
        return carry

    lax.fori_loop(0, 16, gather, 0)
    ready()
    apart = offsets_c_minus_x(False)
    mine = pl.ds(pl.multiple_of(16 * me, 16), 16)

    def windows_of(target):
        acc = jnp.zeros((2 * lines, 256), F32)
        for k in range(16):
            acc = acc + jnp.dot(
                pairs[k], shear_tile(sines, 2 * target, 2 * k, apart, False), preferred_element_type=F32
            )
        mirror = flipped(jnp.concatenate([acc[lines:, :128], acc[lines:, 128:]], axis=0), flip)
        both = (acc[:lines, :128] + mirror[:lines], acc[:lines, 128:] + mirror[lines:])
        return [half.astype(BF16).reshape(lines // 16, 16, 128) for half in both]

    def copy_of(step):
        d = jnp.where(step % 2 == 0, 4 + step // 2, 4 - (step + 1) // 2)
        target = (me + d) % groups
        return target, remote(
            sent.at[step], out_ref.at[:, :, mine, :], send_sems.at[step], recv_sems.at[step], (target, tile)
        )

    def project(step, carry):
        target, copy = copy_of(step)
        both = windows_of(target)
        for t in range(2):
            sent[step, t] = both[t]
        copy.start()
        return carry

    lax.fori_loop(0, groups - 1, project, 0)
    both = windows_of(me)
    for t in range(2):
        out_ref[t, :, mine, :] = both[t]

    def share(slab, k):
        at = pl.ds(pl.multiple_of(16 * slab, 16), 16)
        return remote(
            out_ref.at[:, :, at, :], pair_ref.at[:, :, at, :], pair_sems.at[0, k], pair_sems.at[1, k], sibling
        )

    def came_from(step):
        d = jnp.where(step % 2 == 0, 4 + step // 2, 4 - (step + 1) // 2)
        return (me + groups - d) % groups

    share(me, groups - 1).start()

    def forward(step, carry):
        copy_of(step)[1].wait_recv()
        share(came_from(step), step).start()
        return carry

    lax.fori_loop(0, groups - 1, forward, 0)

    def finish(step, carry):
        copy_of(step)[1].wait_send()
        share(came_from(step), step).wait()
        return carry

    lax.fori_loop(0, groups - 1, finish, 0)
    share(me, groups - 1).wait()


def ring_devices():
    z, tile = lax.axis_index("tilt"), lax.axis_index("tile")
    x, y, c = tile // 8, (tile // 2) % 4, tile % 2

    def dev(dx, dy):
        return (z, ((x + dx) % 4) * 8 + ((y + dy) % 4) * 2 + c)

    right = (dev(1, 0), dev(0, 1))
    left = (dev(3, 0), dev(0, 3))
    sibling = (z, x * 8 + y * 2 + 1 - c)
    return right, left, sibling, (z, (tile + 1) % 32), (z, (tile + 31) % 32)


def image_part(
    defocus, rows_a, cols_a, rows_b, cols_b, win_a, win_b, measured, residual, img, spread_wide, spread,
    shifted, select, loc, s_b, o_b, f_b, s_c, o_c, f_c, table, pred_half, pred, halo, m_halo, res,
    b_sems, c_sems, h_sems, g_sems,
):
    z, tile = lax.axis_index("tilt"), lax.axis_index("tile")
    x, y, c = tile // 8, (tile // 2) % 4, tile % 2
    rights, lefts, sibling, below, above = ring_devices()
    right = lambda axis: rights[axis]
    left = lambda axis: lefts[axis]
    place = (x, y)
    steps = (2, 1, 3, 0)
    m_copies = []
    for k, (device, start) in enumerate(((below, 120), (above, 0))):
        copy = remote(
            measured.at[:, pl.ds(start, 8), :], m_halo.at[k], h_sems.at[0, k], h_sems.at[1, k], device
        )
        copy.start()
        m_copies.append(copy)

    down = lax.broadcasted_iota(jnp.int32, (16, 128), 0).astype(F32)
    along = lax.broadcasted_iota(jnp.int32, (16, 128), 1).astype(F32)
    rho_sq = down * down + along * along
    scale = float(HR * HR)
    for t in range(2):
        spread_wide[t] = jnp.exp(-rho_sq / (2.0 * scale)) * jnp.cos(defocus[0, t] * rho_sq) / scale
    to_scalars = pltpu.make_async_copy(spread_wide, spread, h_sems.at[0, 4])
    to_scalars.start()

    def fill(i, carry):
        lanes = lax.broadcasted_iota(jnp.int32, (16, 256), 1)
        subs = lax.broadcasted_iota(jnp.int32, (16, 256), 0) + i * 16
        apart = jnp.abs(lanes - subs).astype(F32).astype(BF16)
        masks = [apart == jnp.full((16, 256), j, F32).astype(BF16) for j in range(HR + 1)]
        for t in range(2):
            for a in range(HR + 1):
                value = jnp.zeros((16, 256), BF16)
                for j in range(HR + 1):
                    value = jnp.where(masks[j], jnp.full((16, 256), spread[t, a, j], F32).astype(BF16), value)
                table[t, a, pl.ds(pl.multiple_of(i * 16, 16), 16), :] = value
        return carry


    pending = []

    def go(src, dst, sems, t, k, device):
        copy = remote(src, dst, sems.at[0, t, k], sems.at[1, t, k], device)
        copy.start()
        pending.append(copy)
        return copy

    def at_place(t, p, q):
        return (p, q) if t == 0 else (q, p)

    boxes = win_a.shape[1]
    items = [(win_a, rows_a, cols_a, i) for i in range(boxes)] + [(win_b, rows_b, cols_b, i) for i in range(boxes)]
    left_by = lax.broadcasted_iota(jnp.int32, (128, 256), 1) - lax.broadcasted_iota(jnp.int32, (128, 256), 0)
    left_by = left_by.astype(F32).astype(BF16)
    down_by = lax.broadcasted_iota(jnp.int32, (128, 128), 0) - lax.broadcasted_iota(jnp.int32, (128, 128), 1)
    down_by = down_by.astype(F32).astype(BF16)

    def shift_columns(t):
        for i, (windows, _, cols_ref, b) in enumerate(items):
            col = jnp.full((128, 256), cols_ref[t, b].astype(F32), F32).astype(BF16)
            onto = jnp.where(left_by == col, 1.0, 0.0).astype(BF16)
            moved = jnp.dot(windows[t, b], onto, preferred_element_type=F32)
            shifted[t, pl.ds(128 * i, 128), :] = moved.astype(BF16)

    def canvas(t, k):
        p = (place[t] + steps[k]) % 4
        for q in range(4):
            bx, by = at_place(t, p, q)
            top = (bx * 8 + by * 2 + c) * 128
            for i, (_, rows_ref, _, b) in enumerate(items):
                row = jnp.clip(rows_ref[t, b] - top, -128, 128)
                row = jnp.full((128, 128), row.astype(F32), F32).astype(BF16)
                select[t, pl.ds(128 * q, 128), pl.ds(128 * i, 128)] = jnp.where(down_by == row, 1.0, 0.0).astype(BF16)
        return jnp.dot(select[t], shifted[t], preferred_element_type=F32).reshape(4, 128, 256)

    b_in = {}
    for t in range(2):
        shift_columns(t)
        s_b[t, 0] = canvas(t, 0).astype(BF16)
        for h, device in ((0, right(t)), (1, left(t))):
            b_in[t, "opp", h] = go(s_b.at[t, 0, pl.ds(2 * h, 2)], o_b.at[t, h], b_sems, t, h, device)
    for t in range(2):
        for k, h, device in ((1, 1, right(t)), (2, 0, left(t))):
            loc[t, k - 1] = canvas(t, k)
            at = pl.ds(2 * h, 2)
            s_b[t, k, at] = loc[t, k - 1, at].astype(BF16)
            b_in[t, "free", k] = go(s_b.at[t, k, at], f_b.at[t, k - 1, at], b_sems, t, 1 + k, device)
    for t in range(2):
        for k, h, device in ((1, 0, right(t)), (2, 1, left(t))):
            at = pl.ds(2 * h, 2)
            b_in[t, "opp", h].wait_recv()
            s_b[t, k, at] = (loc[t, k - 1, at] + o_b[t, h].astype(F32)).astype(BF16)
            b_in[t, "bound", k] = go(s_b.at[t, k, at], f_b.at[t, k - 1, at], b_sems, t, 3 + k, device)
    for t in range(2):
        loc[t, 2] = canvas(t, 3)
    to_scalars.wait()
    lax.fori_loop(0, 16, fill, 0)
    for t in range(2):
        for k in (1, 2):
            b_in[t, "free", k].wait_recv()
            b_in[t, "bound", k].wait_recv()

    def local_c(t, k, half):
        q = (place[1 - t] + steps[k]) % 4
        at = pl.ds(64 * half, 64)
        return loc[t, 2, q, at, :] + f_b[t, 0, q, at, :].astype(F32) + f_b[t, 1, q, at, :].astype(F32)

    c_in = {}
    for t in range(2):
        for h, device in ((0, right(1 - t)), (1, left(1 - t))):
            at = pl.ds(64 * h, 64)
            s_c[t, 0, at] = local_c(t, 0, h).astype(BF16)
            c_in[t, "opp", h] = go(s_c.at[t, 0, at], o_c.at[t, h], c_sems, t, h, device)
        for k, h, device in ((1, 1, right(1 - t)), (2, 0, left(1 - t))):
            at = pl.ds(64 * h, 64)
            s_c[t, k, at] = local_c(t, k, h).astype(BF16)
            c_in[t, "free", k] = go(s_c.at[t, k, at], f_c.at[t, k - 1, at], c_sems, t, 1 + k, device)
    for t in range(2):
        for k, h, device in ((1, 0, right(1 - t)), (2, 1, left(1 - t))):
            at = pl.ds(64 * h, 64)
            c_in[t, "opp", h].wait_recv()
            s_c[t, k, at] = (local_c(t, k, h) + o_c[t, h].astype(F32)).astype(BF16)
            c_in[t, "bound", k] = go(s_c.at[t, k, at], f_c.at[t, k - 1, at], c_sems, t, 3 + k, device)
    for t in range(2):
        for k in (1, 2):
            c_in[t, "free", k].wait_recv()
            c_in[t, "bound", k].wait_recv()
        total = jnp.concatenate([local_c(t, 3, h) for h in range(2)], axis=0)
        total = total + f_c[t, 0].astype(F32) + f_c[t, 1].astype(F32)
        pred_half[t] = total.astype(BF16)
        pred[t, pl.ds(16, 128), :] = pred_half[t].astype(F32)

    p_copies = []
    for k, (device, start) in enumerate(((below, 112), (above, 0))):
        copy = remote(
            pred_half.at[:, pl.ds(start, 16), :], halo.at[k], h_sems.at[0, 2 + k], h_sems.at[1, 2 + k], device
        )
        copy.start()
        p_copies.append(copy)
    has_above = jnp.where(tile > 0, 1.0, 0.0).astype(F32)
    has_below = jnp.where(tile < 31, 1.0, 0.0).astype(F32)
    for copy in m_copies + p_copies:
        copy.wait_recv()
    for t in range(2):
        pred[t, pl.ds(0, 16), :] = halo[0, t].astype(F32) * has_above
        pred[t, pl.ds(144, 16), :] = halo[1, t].astype(F32) * has_below

    g_in = {}

    def give(t, bx, by, core, rows, k, device):
        top = (bx * 8 + by * 2 + core) * 128 + rows[0]
        where = img.at[t, pl.ds(pl.multiple_of(top, 64), rows[1]), :]
        copy = remote(where, where, g_sems.at[0, t, k], g_sems.at[1, t, k], device)
        copy.start()
        pending.append(copy)
        return copy

    for t in range(2):
        total = jnp.zeros((144, 256), F32)
        for i in range(2 * HR + 1):
            lhs = pred[t, pl.ds(i, 144), :].astype(BF16)
            total = total + jnp.dot(lhs, table[t, abs(i - HR)], preferred_element_type=F32)
        inner = measured[t] - total[8:136]
        residual[t] = inner
        res[t, pl.ds(8, 128), :] = inner.astype(BF16).astype(F32)
        res[t, pl.ds(0, 8), :] = (m_halo[0, t] - total[0:8]).astype(BF16).astype(F32) * has_above
        res[t, pl.ds(136, 8), :] = (m_halo[1, t] - total[136:144]).astype(BF16).astype(F32) * has_below
        total = jnp.zeros((128, 256), F32)
        for i in range(2 * HR + 1):
            lhs = res[t, pl.ds(i, 128), :].astype(BF16)
            total = total + jnp.dot(lhs, table[t, abs(i - HR)], preferred_element_type=F32)
        img[t, pl.ds(pl.multiple_of(tile * 128, 128), 128), :] = total.astype(BF16)
        whole = (0, 128)
        g_in[t, "q", 0] = give(t, x, y, c, whole, 0, right(1 - t))
        g_in[t, "q", 1] = give(t, x, y, c, whole, 1, left(1 - t))
        g_in[t, "p", 0, 0] = give(t, x, y, c, whole, 4, right(t))
        g_in[t, "p", 0, 1] = give(t, x, y, c, whole, 5, left(t))
        g_in[t, "s", 0, 0] = give(t, x, y, c, whole, 20, sibling)

    def spread_block(t, dq, slot):
        q = (place[1 - t] + dq) % 4
        bx, by = at_place(t, place[t], q)
        g_in[t, "p", slot, 0] = give(t, bx, by, c, (0, 128), 4 + 4 * slot, right(t))
        g_in[t, "p", slot, 1] = give(t, bx, by, c, (0, 128), 5 + 4 * slot, left(t))
        g_in[t, "s", 0, slot] = give(t, bx, by, c, (0, 128), 20 + slot, sibling)

    for t in range(2):
        g_in[t, "q", 0].wait_recv()
        bx, by = at_place(t, place[t], (place[1 - t] + 3) % 4)
        g_in[t, "q", 2] = give(t, bx, by, c, (0, 64), 2, right(1 - t))
        g_in[t, "q", 1].wait_recv()
        bx2, by2 = at_place(t, place[t], (place[1 - t] + 1) % 4)
        g_in[t, "q", 3] = give(t, bx2, by2, c, (64, 64), 3, left(1 - t))
        spread_block(t, 3, 1)
        spread_block(t, 1, 2)
    for t in range(2):
        g_in[t, "q", 2].wait_recv()
        g_in[t, "q", 3].wait_recv()
        spread_block(t, 2, 3)

    offsets = (0, 3, 1, 2)
    for slot in range(4):
        for t in range(2):
            q = (place[1 - t] + offsets[slot]) % 4
            for side, (dp, start, device) in enumerate(((3, 0, right(t)), (1, 64, left(t)))):
                g_in[t, "p", slot, side].wait_recv()
                bx, by = at_place(t, (place[t] + dp) % 4, q)
                g_in[t, "f", slot, side] = give(t, bx, by, c, (start, 64), 6 + 4 * slot + side, device)
                g_in[t, "s", 1 + side, slot] = give(t, bx, by, c, (0, 128), 24 + 4 * side + slot, sibling)
    for slot in range(4):
        for t in range(2):
            q = (place[1 - t] + offsets[slot]) % 4
            g_in[t, "f", slot, 0].wait_recv()
            g_in[t, "f", slot, 1].wait_recv()
            bx, by = at_place(t, (place[t] + 2) % 4, q)
            g_in[t, "s", 3, slot] = give(t, bx, by, c, (0, 128), 32 + slot, sibling)
    for slot in range(4):
        for t in range(2):
            for column in range(4):
                g_in[t, "s", column, slot].wait_recv()
    for copy in m_copies + p_copies + pending:
        copy.wait_send()


def cut_part(rows_ref, cols_ref, img, out_ref):
    tilts, boxes = out_ref.shape[:2]
    count = img.shape[1] // 128
    apart = lambda n, m: (
        lax.broadcasted_iota(jnp.int32, (n, m), 0) - lax.broadcasted_iota(jnp.int32, (n, m), 1)
    ).astype(F32).astype(BF16)
    down_by, left_by = apart(128, 256), apart(256, 128)
    fill = lambda value, n, m: jnp.full((n, m), value.astype(F32), F32).astype(BF16)
    for t in range(tilts):
        for b in range(boxes):
            row, col = rows_ref[t, b], cols_ref[t, b]
            home = row // 128
            first, second = fill(home, 128, 256), fill(home + 1, 128, 256)

            def choose(strip, both):
                block = img[t, pl.ds(pl.multiple_of(strip * 128, 128), 128), :]
                here = fill(strip, 128, 256)
                return jnp.where(first == here, block, both[0]), jnp.where(second == here, block, both[1])

            nothing = jnp.zeros((128, 256), BF16)
            rough = jnp.concatenate(lax.fori_loop(0, count, choose, (nothing, nothing), unroll=2), axis=0)
            pick = jnp.where(down_by == fill(home * 128 - row, 128, 256), 1.0, 0.0).astype(BF16)
            lines = jnp.dot(pick, rough, preferred_element_type=F32).astype(BF16)
            pick = jnp.where(left_by == fill(col, 256, 128), 1.0, 0.0).astype(BF16)
            out_ref[t, b] = jnp.dot(lines, pick, preferred_element_type=F32).astype(BF16)


ORDER = ((0, 1), (7, 2), (6, 3), (5, 4))


def layer_product(lines, sines, groups_of, layer, apart):
    acc = jnp.zeros((lines.shape[1], 256), F32)
    for slot in range(2):
        weights = shear_tile(sines, 2 * groups_of[slot], layer, apart, True)
        acc = acc + jnp.dot(lines[slot], weights, preferred_element_type=F32)
    return acc


def back_part(groups, me, tile, sines, windows, sums_hbm, lines_hbm, got, lines, sums, send_sems, recv_sems, sems):
    flip = flip_matrix()
    count = lines.shape[1] // 2
    copies = {}
    for d in (1, 7, 2, 6, 3, 5, 4):
        target = (me + d) % groups
        copies[d] = remote(
            windows.at[:, :, pl.ds(pl.multiple_of(16 * target, 16), 16), :], got.at[d],
            send_sems.at[d], recv_sems.at[d], (target, tile),
        )
        copies[d].start()
    apart = offsets_c_minus_x(True)

    def take(slot, rows):
        for t in range(2):
            at = pl.ds(128 * t, 128)
            line = rows[t].reshape(count, 128)
            lines[slot, pl.ds(0, count), at] = line
            lines[slot, pl.ds(count, count), at] = jnp.dot(line, flip, preferred_element_type=F32).astype(BF16)

    def out_copy(i):
        at = pl.ds(4 * i, 4)
        return pltpu.make_async_copy(sums.at[at], sums_hbm.at[at], sems.at[i])

    for stage, pair in enumerate(ORDER):
        for slot, d in enumerate(pair):
            if d == 0:
                take(slot, windows[:, :, pl.ds(pl.multiple_of(16 * me, 16), 16), :])
            else:
                copies[d].wait_recv()
                take(slot, got[d])
        if stage == 3:
            break
        from_group = [(me - d + groups) % groups for d in pair]

        def add(i, carry):
            for k in range(4):
                value = layer_product(lines, sines, from_group, 8 * i + 2 * k, apart)
                sums[4 * i + k] = value if stage == 0 else sums[4 * i + k] + value
            if stage == 2:
                out_copy(i).start()
            return carry

        lax.fori_loop(0, 4, add, 0)
    last = pltpu.make_async_copy(lines, lines_hbm, sems.at[4])
    last.start()

    def finish(i, carry):
        out_copy(i).wait()
        return carry

    lax.fori_loop(0, 4, finish, 0)
    last.wait()
    for copy in copies.values():
        copy.wait_send()


def finish_kernel(
    groups, angles_hbm, lines_hbm, sums_hbm, residual_hbm, residual, out_ref,
    angles, sines, lines, sums, blocks, load_sems, sems,
):
    me = lax.axis_index("tilt")

    def sums_copy(i):
        at = pl.ds(4 * i, 4)
        return pltpu.make_async_copy(sums_hbm.at[at], sums.at[at], load_sems.at[i])

    smalls = [
        pltpu.make_async_copy(src, dst, load_sems.at[4 + k])
        for k, (src, dst) in enumerate(((angles_hbm, angles), (lines_hbm, lines), (residual_hbm, residual)))
    ]
    smalls[0].start()
    smalls[1].start()
    for i in range(4):
        sums_copy(i).start()
    smalls[2].start()
    smalls[0].wait()
    for t in range(sines.shape[0]):
        sines[t] = sine(angles[0, t])
    smalls[1].wait()
    flip = flip_matrix()
    apart = offsets_c_minus_x(True)
    count = lines.shape[1] // 2
    scale = 1.0 / (2 * groups)
    from_group = [(me - d + groups) % groups for d in ORDER[-1]]

    def copies_of(i):
        low = pltpu.make_async_copy(
            blocks.at[0, i], out_ref.at[:, pl.ds(pl.multiple_of(8 * i, 8), 8), :], sems.at[0, i]
        )
        high = pltpu.make_async_copy(
            blocks.at[1, i], out_ref.at[:, pl.ds(pl.multiple_of(56 - 8 * i, 8), 8), :], sems.at[1, i]
        )
        return low, high

    def layers(i, carry):
        sums_copy(i).wait()
        for k in range(4):
            acc = (sums[4 * i + k] + layer_product(lines, sines, from_group, 8 * i + 2 * k, apart)) * scale
            blocks[0, i, :, 2 * k, :] = acc[:count, :128]
            blocks[0, i, :, 2 * k + 1, :] = acc[:count, 128:]
            mirror = flipped(jnp.concatenate([acc[count:, :128], acc[count:, 128:]], axis=0), flip)
            blocks[1, i, :, 7 - 2 * k, :] = mirror[:count]
            blocks[1, i, :, 6 - 2 * k, :] = mirror[count:]
        for copy in copies_of(i):
            copy.start()
        return carry

    lax.fori_loop(0, 4, layers, 0)

    def finish(i, carry):
        for copy in copies_of(i):
            copy.wait()
        return carry

    lax.fori_loop(0, 4, finish, 0)
    smalls[2].wait()


def whole_kernel(
    groups, angles_hbm, rows_hbm, cols_hbm, defocus_hbm, v_hbm, m_hbm, residual_hbm, sums_hbm, lines_hbm,
    angles, sines, rows, cols, defocus, rows_b, cols_b, rows_v, cols_v, rows_bv, cols_bv, v_ref, measured,
    residual, windows, windows_b, img, back_windows, load_sems, v_sems, note_sems, *rest
):
    project_refs, image_refs, back_refs = rest[:6], rest[6:-6], rest[-6:]
    me, tile = lax.axis_index("tilt"), lax.axis_index("tile")
    rights, lefts, sibling, below, above = ring_devices()
    smalls = [
        pltpu.make_async_copy(src, dst, load_sems.at[k])
        for k, (src, dst) in enumerate((
            (angles_hbm, angles), (rows_hbm, rows_v), (cols_hbm, cols_v), (rows_hbm, rows), (cols_hbm, cols),
            (defocus_hbm, defocus), (m_hbm, measured),
        ))
    ]
    parts = v_sems.shape[0]
    size = v_ref.shape[0] // parts
    loads = []
    for i in range(parts):
        at = pl.ds(i * size, size)
        loads.append(pltpu.make_async_copy(v_hbm.at[at], v_ref.at[at], v_sems.at[i]))
        loads[-1].start()
    for copy in smalls:
        copy.start()
    partners = [((me + d) % groups, tile) for d in range(1, groups)]
    partners += [sibling, below, above, rights[0], rights[1], lefts[0], lefts[1]]
    for device in partners:
        signal(device)
    smalls[0].wait()
    for t in range(sines.shape[0]):
        sines[t] = sine(angles[0, t])
    notes = [
        remote(src, dst, note_sems.at[0, k], note_sems.at[1, k], sibling)
        for k, (src, dst) in enumerate(((rows_v, rows_bv), (cols_v, cols_bv)))
    ]

    def ready():
        pl.semaphore_wait(pltpu.get_barrier_semaphore(), len(partners))
        for k in (1, 2):
            smalls[k].wait()
        for copy in notes:
            copy.start()

    project_part(groups, me, tile, sibling, loads, ready, sines, v_ref, windows, windows_b, *project_refs)
    for copy in notes:
        copy.wait()
    into = [
        pltpu.make_async_copy(src, dst, load_sems.at[7 + k])
        for k, (src, dst) in enumerate(((rows_bv, rows_b), (cols_bv, cols_b)))
    ]
    for copy in into:
        copy.start()
    for copy in smalls[3:] + into:
        copy.wait()
    image_part(defocus, rows, cols, rows_b, cols_b, windows, windows_b, measured, residual, img, *image_refs)
    keep = pltpu.make_async_copy(residual, residual_hbm, load_sems.at[9])
    keep.start()
    cut_part(rows, cols, img, back_windows)
    back_part(groups, me, tile, sines, back_windows, sums_hbm, lines_hbm, *back_refs)
    keep.wait()


VMEM = pl.BlockSpec(memory_space=pltpu.VMEM)
HBM = pl.BlockSpec(memory_space=pltpu.HBM)


def call_whole(volumes, angles, defocus, rows, cols, measured, groups):
    boxes, slab, depth, width = volumes.shape
    lines = boxes * slab
    dma = lambda *shape: pltpu.SemaphoreType.DMA(shape)
    blocks = lambda *shape: pltpu.VMEM(shape, BF16)
    floats = lambda *shape: pltpu.VMEM(shape, F32)
    count = 2 * boxes * 128
    whole = [
        pltpu.SMEM((1, 2 * groups), F32),
        pltpu.SMEM((2 * groups,), F32),
        pltpu.SMEM((2, boxes), jnp.int32),
        pltpu.SMEM((2, boxes), jnp.int32),
        pltpu.SMEM((1, 2), F32),
        pltpu.SMEM((2, boxes), jnp.int32),
        pltpu.SMEM((2, boxes), jnp.int32),
        pltpu.VMEM((2, boxes), jnp.int32),
        pltpu.VMEM((2, boxes), jnp.int32),
        pltpu.VMEM((2, boxes), jnp.int32),
        pltpu.VMEM((2, boxes), jnp.int32),
        blocks(lines * depth, width),
        floats(*measured.shape),
        floats(*measured.shape),
        blocks(2, boxes, slab * groups, width),
        blocks(2, boxes, slab * groups, width),
        blocks(2, 4096, 256),
        blocks(2, boxes, slab * groups, width),
        dma(10), dma(4), dma(2, 2),
    ]
    project = [
        floats(lines * depth, width),
        blocks(depth // 4, 2 * lines, 2 * width),
        blocks(groups, 2, boxes, slab, width),
        dma(groups), dma(groups), dma(2, groups),
    ]
    image = [
        floats(2, 16, 128),
        pltpu.SMEM((2, 16, 128), F32),
        blocks(2, count, 256),
        blocks(2, 512, count),
        floats(2, 3, 4, 128, 256),
        blocks(2, 3, 4, 128, 256),
        blocks(2, 2, 2, 128, 256),
        blocks(2, 2, 4, 128, 256),
        blocks(2, 3, 128, 256),
        blocks(2, 2, 64, 256),
        blocks(2, 2, 128, 256),
        blocks(2, 9, 256, 256),
        blocks(2, 128, 256),
        floats(2, 160, 256),
        blocks(2, 2, 16, 256),
        floats(2, 2, 8, 256),
        floats(2, 144, 256),
        dma(2, 2, 6), dma(2, 2, 6), dma(2, 5), dma(2, 2, 36),
    ]
    back = [
        blocks(groups, 2, boxes, slab, width),
        blocks(2, 2 * lines, 2 * width),
        floats(16, 2 * lines, 2 * width),
        dma(groups), dma(groups), dma(5),
    ]
    angles = angles.reshape(1, -1)
    residual, sums, last = pl.pallas_call(
        functools.partial(whole_kernel, groups),
        out_shape=(
            jax.ShapeDtypeStruct(measured.shape, F32),
            jax.ShapeDtypeStruct((16, 2 * lines, 2 * width), F32),
            jax.ShapeDtypeStruct((2, 2 * lines, 2 * width), BF16),
        ),
        in_specs=[HBM] * 6,
        out_specs=(HBM,) * 3,
        scratch_shapes=whole + project + image + back,
        compiler_params=pltpu.CompilerParams(
            collective_id=0, has_side_effects=True, vmem_limit_bytes=56 * MIB
        ),
    )(angles, rows, cols, defocus.reshape(1, -1), volumes.reshape(lines * depth, width), measured)
    residual, step = pl.pallas_call(
        functools.partial(finish_kernel, groups),
        out_shape=(
            jax.ShapeDtypeStruct(measured.shape, F32), jax.ShapeDtypeStruct((lines, depth, width), F32)
        ),
        in_specs=[HBM] * 4,
        out_specs=(HBM,) * 2,
        scratch_shapes=[
            pltpu.SMEM((1, 2 * groups), F32),
            pltpu.SMEM((2 * groups,), F32),
            blocks(2, 2 * lines, 2 * width),
            floats(16, 2 * lines, 2 * width),
            floats(2, 4, lines, 8, width),
            dma(7), dma(2, 4),
        ],
        compiler_params=pltpu.CompilerParams(vmem_limit_bytes=56 * MIB),
    )(angles, last, sums, residual)
    return residual, step.reshape(volumes.shape)


def shards(volumes, angles, defocus, row_offsets, col_offsets, measured):
    return call_whole(
        volumes, angles, defocus, row_offsets.T, col_offsets.T, measured, lax.axis_size("tilt")
    )


def solution(mesh):
    in_specs = (
        P("tile", "tilt", None, None),
        P(),
        P("tilt"),
        P("tile", "tilt"),
        P("tile", "tilt"),
        P("tilt", "tile", None),
    )
    out_specs = (P("tilt", "tile", None), P("tile", "tilt", None, None))
    return jax.shard_map(shards, mesh=mesh, in_specs=in_specs, out_specs=out_specs, check_vma=False)
```

```python
import functools

import jax
import jax.numpy as jnp
from jax import lax
from jax.experimental import pallas as pl
from jax.experimental.pallas import tpu as pltpu
from jax.sharding import PartitionSpec as P

HR = 8
MESH = pl.DeviceIdType.MESH
BF16 = jnp.bfloat16
F32 = jnp.float32
MIB = 1 << 20


def signal(device):
    pl.semaphore_signal(
        pltpu.get_barrier_semaphore(), inc=1, device_id=device, device_id_type=MESH
    )


def remote(src, dst, send_sem, recv_sem, device):
    return pltpu.make_async_remote_copy(
        src_ref=src, dst_ref=dst, send_sem=send_sem, recv_sem=recv_sem,
        device_id=device, device_id_type=MESH,
    )


def offsets_c_minus_x(transposed):
    rows = lax.broadcasted_iota(jnp.int32, (128, 128), 0)
    cols = lax.broadcasted_iota(jnp.int32, (128, 128), 1)
    return ((rows - cols) if transposed else (cols - rows)).astype(F32).astype(BF16)


def sine(x):
    square = x * x
    value = -1.0 / 39916800.0 + square * (1.0 / 6227020800.0)
    for factor in (1.0 / 362880.0, -1.0 / 5040.0, 1.0 / 120.0, -1.0 / 6.0):
        value = factor + square * value
    return x + x * (square * value)


def shear_block(sines, tilt, layer, apart):
    shift = (jnp.asarray(layer, jnp.int32).astype(F32) - 31.5) * sines[tilt]
    tap = shift.astype(jnp.int32).astype(F32)
    tap = jnp.where(tap > shift, tap - 1.0, tap)
    all_of = lambda value: jnp.full((128, 128), value, F32).astype(BF16)
    near = jnp.maximum(0.0, 1.0 - jnp.abs(tap - shift))
    far = jnp.maximum(0.0, 1.0 - jnp.abs(tap + 1.0 - shift))
    zero = jnp.zeros((128, 128), BF16)
    return jnp.where(apart == all_of(tap), all_of(near), jnp.where(apart == all_of(tap + 1.0), all_of(far), zero))


def shear_tile(sines, tilt, layer, apart, transposed):
    make = lambda t, z: shear_block(sines, tilt + t, layer + z, apart)
    if transposed:
        parts = [[make(t, z) for z in range(2)] for t in range(2)]
    else:
        parts = [[make(t, z) for t in range(2)] for z in range(2)]
    return jnp.concatenate([jnp.concatenate(row, axis=1) for row in parts], axis=0)


def flip_matrix():
    rows = lax.broadcasted_iota(jnp.int32, (128, 128), 0)
    cols = lax.broadcasted_iota(jnp.int32, (128, 128), 1)
    return jnp.where(rows + cols == 127, 1.0, 0.0).astype(BF16)


def flipped(x, flip):
    high = x.astype(BF16)
    low = (x - high.astype(F32)).astype(BF16)
    return jnp.dot(
        jnp.concatenate([high, low], axis=1), jnp.concatenate([flip, flip], axis=0), preferred_element_type=F32
    )


def project_part(
    groups, me, tile, sibling, loads, ready, sines, v_ref, out_ref, pair_ref,
    wide, pairs, sent, send_sems, recv_sems, pair_sems,
):
    rows = v_ref.shape[0]
    lines = rows // 64
    parts = len(loads)
    size = rows // parts

    def widen(i, carry):
        at = pl.ds(pl.multiple_of(i * 512, 512), 512)
        wide[at, :] = v_ref[at, :].astype(F32)
        return carry

    for i in range(parts):
        loads[i].wait()
        lax.fori_loop(i * size // 512, (i + 1) * size // 512, widen, 0)
    flip = flip_matrix()

    def gather(k, carry):
        layer = lambda z: wide[pl.ds(z, lines, stride=64), :]
        top = jnp.concatenate([layer(2 * k), layer(2 * k + 1)], axis=1).astype(BF16)
        mirror = jnp.concatenate([layer(63 - 2 * k), layer(62 - 2 * k)], axis=0).astype(BF16)
        mirror = jnp.dot(mirror, flip, preferred_element_type=F32).astype(BF16)
        pairs[k] = jnp.concatenate([top, jnp.concatenate([mirror[:lines], mirror[lines:]], axis=1)], axis=0)
        return carry

    lax.fori_loop(0, 16, gather, 0)
    ready()
    apart = offsets_c_minus_x(False)
    mine = pl.ds(pl.multiple_of(16 * me, 16), 16)

    def windows_of(target):
        acc = jnp.zeros((2 * lines, 256), F32)
        for k in range(16):
            acc = acc + jnp.dot(
                pairs[k], shear_tile(sines, 2 * target, 2 * k, apart, False), preferred_element_type=F32
            )
        mirror = flipped(jnp.concatenate([acc[lines:, :128], acc[lines:, 128:]], axis=0), flip)
        both = (acc[:lines, :128] + mirror[:lines], acc[:lines, 128:] + mirror[lines:])
        return [half.astype(BF16).reshape(lines // 16, 16, 128) for half in both]

    def copy_of(step):
        d = jnp.where(step % 2 == 0, 4 + step // 2, 4 - (step + 1) // 2)
        target = (me + d) % groups
        return target, remote(
            sent.at[step], out_ref.at[:, :, mine, :], send_sems.at[step], recv_sems.at[step], (target, tile)
        )

    def project(step, carry):
        target, copy = copy_of(step)
        both = windows_of(target)
        for t in range(2):
            sent[step, t] = both[t]
        copy.start()
        return carry

    lax.fori_loop(0, groups - 1, project, 0)
    both = windows_of(me)
    for t in range(2):
        out_ref[t, :, mine, :] = both[t]

    def share(slab, k):
        at = pl.ds(pl.multiple_of(16 * slab, 16), 16)
        return remote(
            out_ref.at[:, :, at, :], pair_ref.at[:, :, at, :], pair_sems.at[0, k], pair_sems.at[1, k], sibling
        )

    def came_from(step):
        d = jnp.where(step % 2 == 0, 4 + step // 2, 4 - (step + 1) // 2)
        return (me + groups - d) % groups

    share(me, groups - 1).start()

    def forward(step, carry):
        copy_of(step)[1].wait_recv()
        share(came_from(step), step).start()
        return carry

    lax.fori_loop(0, groups - 1, forward, 0)

    def finish(step, carry):
        copy_of(step)[1].wait_send()
        share(came_from(step), step).wait()
        return carry

    lax.fori_loop(0, groups - 1, finish, 0)
    share(me, groups - 1).wait()


def ring_devices():
    z, tile = lax.axis_index("tilt"), lax.axis_index("tile")
    x, y, c = tile // 8, (tile // 2) % 4, tile % 2

    def dev(dx, dy):
        return (z, ((x + dx) % 4) * 8 + ((y + dy) % 4) * 2 + c)

    right = (dev(1, 0), dev(0, 1))
    left = (dev(3, 0), dev(0, 3))
    sibling = (z, x * 8 + y * 2 + 1 - c)
    return right, left, sibling, (z, (tile + 1) % 32), (z, (tile + 31) % 32)


def image_part(
    defocus, rows_a, cols_a, rows_b, cols_b, win_a, win_b, measured, residual, img, spread_wide, spread,
    shifted, select, loc, s_b, o_b, f_b, s_c, o_c, f_c, table, pred_half, pred, halo, m_halo, res,
    b_sems, c_sems, h_sems, g_sems,
):
    z, tile = lax.axis_index("tilt"), lax.axis_index("tile")
    x, y, c = tile // 8, (tile // 2) % 4, tile % 2
    rights, lefts, sibling, below, above = ring_devices()
    right = lambda axis: rights[axis]
    left = lambda axis: lefts[axis]
    place = (x, y)
    steps = (2, 1, 3, 0)
    m_copies = []
    for k, (device, start) in enumerate(((below, 120), (above, 0))):
        copy = remote(
            measured.at[:, pl.ds(start, 8), :], m_halo.at[k], h_sems.at[0, k], h_sems.at[1, k], device
        )
        copy.start()
        m_copies.append(copy)

    down = lax.broadcasted_iota(jnp.int32, (16, 128), 0).astype(F32)
    along = lax.broadcasted_iota(jnp.int32, (16, 128), 1).astype(F32)
    rho_sq = down * down + along * along
    scale = float(HR * HR)
    for t in range(2):
        spread_wide[t] = jnp.exp(-rho_sq / (2.0 * scale)) * jnp.cos(defocus[0, t] * rho_sq) / scale
    to_scalars = pltpu.make_async_copy(spread_wide, spread, h_sems.at[0, 4])
    to_scalars.start()

    def fill(i, carry):
        lanes = lax.broadcasted_iota(jnp.int32, (16, 256), 1)
        subs = lax.broadcasted_iota(jnp.int32, (16, 256), 0) + i * 16
        apart = jnp.abs(lanes - subs).astype(F32).astype(BF16)
        masks = [apart == jnp.full((16, 256), j, F32).astype(BF16) for j in range(HR + 1)]
        for t in range(2):
            for a in range(HR + 1):
                value = jnp.zeros((16, 256), BF16)
                for j in range(HR + 1):
                    value = jnp.where(masks[j], jnp.full((16, 256), spread[t, a, j], F32).astype(BF16), value)
                table[t, a, pl.ds(pl.multiple_of(i * 16, 16), 16), :] = value
        return carry


    pending = []

    def go(src, dst, sems, t, k, device):
        copy = remote(src, dst, sems.at[0, t, k], sems.at[1, t, k], device)
        copy.start()
        pending.append(copy)
        return copy

    def at_place(t, p, q):
        return (p, q) if t == 0 else (q, p)

    boxes = win_a.shape[1]
    items = [(win_a, rows_a, cols_a, i) for i in range(boxes)] + [(win_b, rows_b, cols_b, i) for i in range(boxes)]
    left_by = lax.broadcasted_iota(jnp.int32, (128, 256), 1) - lax.broadcasted_iota(jnp.int32, (128, 256), 0)
    left_by = left_by.astype(F32).astype(BF16)
    down_by = lax.broadcasted_iota(jnp.int32, (128, 128), 0) - lax.broadcasted_iota(jnp.int32, (128, 128), 1)
    down_by = down_by.astype(F32).astype(BF16)

    def shift_columns(t):
        for i, (windows, _, cols_ref, b) in enumerate(items):
            col = jnp.full((128, 256), cols_ref[t, b].astype(F32), F32).astype(BF16)
            onto = jnp.where(left_by == col, 1.0, 0.0).astype(BF16)
            moved = jnp.dot(windows[t, b], onto, preferred_element_type=F32)
            shifted[t, pl.ds(128 * i, 128), :] = moved.astype(BF16)

    def canvas(t, k):
        p = (place[t] + steps[k]) % 4
        for q in range(4):
            bx, by = at_place(t, p, q)
            top = (bx * 8 + by * 2 + c) * 128
            for i, (_, rows_ref, _, b) in enumerate(items):
                row = jnp.clip(rows_ref[t, b] - top, -128, 128)
                row = jnp.full((128, 128), row.astype(F32), F32).astype(BF16)
                select[t, pl.ds(128 * q, 128), pl.ds(128 * i, 128)] = jnp.where(down_by == row, 1.0, 0.0).astype(BF16)
        return jnp.dot(select[t], shifted[t], preferred_element_type=F32).reshape(4, 128, 256)

    b_in = {}
    for t in range(2):
        shift_columns(t)
        s_b[t, 0] = canvas(t, 0).astype(BF16)
        for h, device in ((0, right(t)), (1, left(t))):
            b_in[t, "opp", h] = go(s_b.at[t, 0, pl.ds(2 * h, 2)], o_b.at[t, h], b_sems, t, h, device)
    for t in range(2):
        for k, h, device in ((1, 1, right(t)), (2, 0, left(t))):
            loc[t, k - 1] = canvas(t, k)
            at = pl.ds(2 * h, 2)
            s_b[t, k, at] = loc[t, k - 1, at].astype(BF16)
            b_in[t, "free", k] = go(s_b.at[t, k, at], f_b.at[t, k - 1, at], b_sems, t, 1 + k, device)
    for t in range(2):
        for k, h, device in ((1, 0, right(t)), (2, 1, left(t))):
            at = pl.ds(2 * h, 2)
            b_in[t, "opp", h].wait_recv()
            s_b[t, k, at] = (loc[t, k - 1, at] + o_b[t, h].astype(F32)).astype(BF16)
            b_in[t, "bound", k] = go(s_b.at[t, k, at], f_b.at[t, k - 1, at], b_sems, t, 3 + k, device)
    for t in range(2):
        loc[t, 2] = canvas(t, 3)
    to_scalars.wait()
    lax.fori_loop(0, 16, fill, 0)
    for t in range(2):
        for k in (1, 2):
            b_in[t, "free", k].wait_recv()
            b_in[t, "bound", k].wait_recv()

    def local_c(t, k, half):
        q = (place[1 - t] + steps[k]) % 4
        at = pl.ds(64 * half, 64)
        return loc[t, 2, q, at, :] + f_b[t, 0, q, at, :].astype(F32) + f_b[t, 1, q, at, :].astype(F32)

    c_in = {}
    for t in range(2):
        for h, device in ((0, right(1 - t)), (1, left(1 - t))):
            at = pl.ds(64 * h, 64)
            s_c[t, 0, at] = local_c(t, 0, h).astype(BF16)
            c_in[t, "opp", h] = go(s_c.at[t, 0, at], o_c.at[t, h], c_sems, t, h, device)
        for k, h, device in ((1, 1, right(1 - t)), (2, 0, left(1 - t))):
            at = pl.ds(64 * h, 64)
            s_c[t, k, at] = local_c(t, k, h).astype(BF16)
            c_in[t, "free", k] = go(s_c.at[t, k, at], f_c.at[t, k - 1, at], c_sems, t, 1 + k, device)
    for t in range(2):
        for k, h, device in ((1, 0, right(1 - t)), (2, 1, left(1 - t))):
            at = pl.ds(64 * h, 64)
            c_in[t, "opp", h].wait_recv()
            s_c[t, k, at] = (local_c(t, k, h) + o_c[t, h].astype(F32)).astype(BF16)
            c_in[t, "bound", k] = go(s_c.at[t, k, at], f_c.at[t, k - 1, at], c_sems, t, 3 + k, device)
    for t in range(2):
        for k in (1, 2):
            c_in[t, "free", k].wait_recv()
            c_in[t, "bound", k].wait_recv()
        total = jnp.concatenate([local_c(t, 3, h) for h in range(2)], axis=0)
        total = total + f_c[t, 0].astype(F32) + f_c[t, 1].astype(F32)
        pred_half[t] = total.astype(BF16)
        pred[t, pl.ds(16, 128), :] = pred_half[t].astype(F32)

    p_copies = []
    for k, (device, start) in enumerate(((below, 112), (above, 0))):
        copy = remote(
            pred_half.at[:, pl.ds(start, 16), :], halo.at[k], h_sems.at[0, 2 + k], h_sems.at[1, 2 + k], device
        )
        copy.start()
        p_copies.append(copy)
    has_above = jnp.where(tile > 0, 1.0, 0.0).astype(F32)
    has_below = jnp.where(tile < 31, 1.0, 0.0).astype(F32)
    for copy in m_copies + p_copies:
        copy.wait_recv()
    for t in range(2):
        pred[t, pl.ds(0, 16), :] = halo[0, t].astype(F32) * has_above
        pred[t, pl.ds(144, 16), :] = halo[1, t].astype(F32) * has_below

    g_in = {}

    def give(t, bx, by, core, rows, k, device):
        top = (bx * 8 + by * 2 + core) * 128 + rows[0]
        where = img.at[t, pl.ds(pl.multiple_of(top, 64), rows[1]), :]
        copy = remote(where, where, g_sems.at[0, t, k], g_sems.at[1, t, k], device)
        copy.start()
        pending.append(copy)
        return copy

    for t in range(2):
        total = jnp.zeros((144, 256), F32)
        for i in range(2 * HR + 1):
            lhs = pred[t, pl.ds(i, 144), :].astype(BF16)
            total = total + jnp.dot(lhs, table[t, abs(i - HR)], preferred_element_type=F32)
        inner = measured[t] - total[8:136]
        residual[t] = inner
        res[t, pl.ds(8, 128), :] = inner.astype(BF16).astype(F32)
        res[t, pl.ds(0, 8), :] = (m_halo[0, t] - total[0:8]).astype(BF16).astype(F32) * has_above
        res[t, pl.ds(136, 8), :] = (m_halo[1, t] - total[136:144]).astype(BF16).astype(F32) * has_below
        total = jnp.zeros((128, 256), F32)
        for i in range(2 * HR + 1):
            lhs = res[t, pl.ds(i, 128), :].astype(BF16)
            total = total + jnp.dot(lhs, table[t, abs(i - HR)], preferred_element_type=F32)
        img[t, pl.ds(pl.multiple_of(tile * 128, 128), 128), :] = total.astype(BF16)
        whole = (0, 128)
        g_in[t, "q", 0] = give(t, x, y, c, whole, 0, right(1 - t))
        g_in[t, "q", 1] = give(t, x, y, c, whole, 1, left(1 - t))
        g_in[t, "p", 0, 0] = give(t, x, y, c, whole, 4, right(t))
        g_in[t, "p", 0, 1] = give(t, x, y, c, whole, 5, left(t))
        g_in[t, "s", 0, 0] = give(t, x, y, c, whole, 20, sibling)

    def spread_block(t, dq, slot):
        q = (place[1 - t] + dq) % 4
        bx, by = at_place(t, place[t], q)
        g_in[t, "p", slot, 0] = give(t, bx, by, c, (0, 128), 4 + 4 * slot, right(t))
        g_in[t, "p", slot, 1] = give(t, bx, by, c, (0, 128), 5 + 4 * slot, left(t))
        g_in[t, "s", 0, slot] = give(t, bx, by, c, (0, 128), 20 + slot, sibling)

    for t in range(2):
        g_in[t, "q", 0].wait_recv()
        bx, by = at_place(t, place[t], (place[1 - t] + 3) % 4)
        g_in[t, "q", 2] = give(t, bx, by, c, (0, 64), 2, right(1 - t))
        g_in[t, "q", 1].wait_recv()
        bx2, by2 = at_place(t, place[t], (place[1 - t] + 1) % 4)
        g_in[t, "q", 3] = give(t, bx2, by2, c, (64, 64), 3, left(1 - t))
        spread_block(t, 3, 1)
        spread_block(t, 1, 2)
    for t in range(2):
        g_in[t, "q", 2].wait_recv()
        g_in[t, "q", 3].wait_recv()
        spread_block(t, 2, 3)

    offsets = (0, 3, 1, 2)
    for slot in range(4):
        for t in range(2):
            q = (place[1 - t] + offsets[slot]) % 4
            for side, (dp, start, device) in enumerate(((3, 0, right(t)), (1, 64, left(t)))):
                g_in[t, "p", slot, side].wait_recv()
                bx, by = at_place(t, (place[t] + dp) % 4, q)
                g_in[t, "f", slot, side] = give(t, bx, by, c, (start, 64), 6 + 4 * slot + side, device)
                g_in[t, "s", 1 + side, slot] = give(t, bx, by, c, (0, 128), 24 + 4 * side + slot, sibling)
    for slot in range(4):
        for t in range(2):
            q = (place[1 - t] + offsets[slot]) % 4
            g_in[t, "f", slot, 0].wait_recv()
            g_in[t, "f", slot, 1].wait_recv()
            bx, by = at_place(t, (place[t] + 2) % 4, q)
            g_in[t, "s", 3, slot] = give(t, bx, by, c, (0, 128), 32 + slot, sibling)
    for slot in range(4):
        for t in range(2):
            for column in range(4):
                g_in[t, "s", column, slot].wait_recv()
    for copy in m_copies + p_copies + pending:
        copy.wait_send()


def cut_part(rows_ref, cols_ref, img, out_ref, send):
    tilts, boxes = out_ref.shape[:2]
    count = img.shape[1] // 128
    apart = lambda n, m: (
        lax.broadcasted_iota(jnp.int32, (n, m), 0) - lax.broadcasted_iota(jnp.int32, (n, m), 1)
    ).astype(F32).astype(BF16)
    down_by, left_by = apart(128, 256), apart(256, 128)
    fill = lambda value, n, m: jnp.full((n, m), value.astype(F32), F32).astype(BF16)
    for t in range(tilts):
        for b in range(boxes):
            row, col = rows_ref[t, b], cols_ref[t, b]
            home = row // 128
            first, second = fill(home, 16, 256), fill(home + 1, 16, 256)

            def choose(strip, both):
                here = fill(strip, 16, 256)
                masks = [first == here] * 8 + [second == here] * 8
                block = [img[t, pl.ds(pl.multiple_of(strip * 128 + 16 * k, 16), 16), :] for k in range(8)] * 2
                return tuple(jnp.where(*three) for three in zip(masks, block, both))

            nothing = (jnp.zeros((16, 256), BF16),) * 16
            rough = jnp.concatenate(lax.fori_loop(0, count, choose, nothing, unroll=2), axis=0)
            pick = jnp.where(down_by == fill(home * 128 - row, 128, 256), 1.0, 0.0).astype(BF16)
            lines = jnp.dot(pick, rough, preferred_element_type=F32).astype(BF16)
            pick = jnp.where(left_by == fill(col, 256, 128), 1.0, 0.0).astype(BF16)
            out_ref[t, b] = jnp.dot(lines, pick, preferred_element_type=F32).astype(BF16)
        send(t)


ORDER = ((0, 1), (7, 2), (6, 3), (5, 4))


def layer_product(lines, sines, groups_of, layer, apart):
    acc = jnp.zeros((lines.shape[1], 256), F32)
    for slot in range(2):
        weights = shear_tile(sines, 2 * groups_of[slot], layer, apart, True)
        acc = acc + jnp.dot(lines[slot], weights, preferred_element_type=F32)
    return acc


def back_copies(groups, me, tile, windows, got, send_sems, recv_sems):
    copies = {}
    for d in (1, 7, 2, 6, 3, 5, 4):
        target = (me + d) % groups
        for t in range(2):
            copies[t, d] = remote(
                windows.at[t, :, pl.ds(pl.multiple_of(16 * target, 16), 16), :], got.at[d, t],
                send_sems.at[t, d], recv_sems.at[t, d], (target, tile),
            )
    return copies


def back_part(groups, me, sines, copies, windows, sums_hbm, lines_hbm, got, lines, sums, sems):
    flip = flip_matrix()
    count = lines.shape[1] // 2
    apart = offsets_c_minus_x(True)

    def take(slot, rows):
        for t in range(2):
            at = pl.ds(128 * t, 128)
            line = rows[t].reshape(count, 128)
            lines[slot, pl.ds(0, count), at] = line
            lines[slot, pl.ds(count, count), at] = jnp.dot(line, flip, preferred_element_type=F32).astype(BF16)

    def out_copy(i):
        at = pl.ds(4 * i, 4)
        return pltpu.make_async_copy(sums.at[at], sums_hbm.at[at], sems.at[i])

    for stage, pair in enumerate(ORDER):
        for slot, d in enumerate(pair):
            if d == 0:
                take(slot, windows[:, :, pl.ds(pl.multiple_of(16 * me, 16), 16), :])
            else:
                for t in range(2):
                    copies[t, d].wait_recv()
                take(slot, got[d])
        if stage == 3:
            break
        from_group = [(me - d + groups) % groups for d in pair]

        def add(i, carry):
            for k in range(4):
                value = layer_product(lines, sines, from_group, 8 * i + 2 * k, apart)
                sums[4 * i + k] = value if stage == 0 else sums[4 * i + k] + value
            if stage == 2:
                out_copy(i).start()
            return carry

        lax.fori_loop(0, 4, add, 0)
    last = pltpu.make_async_copy(lines, lines_hbm, sems.at[4])
    last.start()

    def finish(i, carry):
        out_copy(i).wait()
        return carry

    lax.fori_loop(0, 4, finish, 0)
    last.wait()
    for copy in copies.values():
        copy.wait_send()


def finish_kernel(
    groups, angles_hbm, lines_hbm, sums_hbm, residual_hbm, residual, out_ref,
    angles, sines, lines, sums, blocks, load_sems, sems,
):
    me = lax.axis_index("tilt")

    def sums_copy(i):
        at = pl.ds(4 * i, 4)
        return pltpu.make_async_copy(sums_hbm.at[at], sums.at[at], load_sems.at[i])

    smalls = [
        pltpu.make_async_copy(src, dst, load_sems.at[4 + k])
        for k, (src, dst) in enumerate(((angles_hbm, angles), (lines_hbm, lines), (residual_hbm, residual)))
    ]
    smalls[0].start()
    smalls[1].start()
    for i in range(4):
        sums_copy(i).start()
    smalls[2].start()
    smalls[0].wait()
    for t in range(sines.shape[0]):
        sines[t] = sine(angles[0, t])
    smalls[1].wait()
    flip = flip_matrix()
    apart = offsets_c_minus_x(True)
    count = lines.shape[1] // 2
    scale = 1.0 / (2 * groups)
    from_group = [(me - d + groups) % groups for d in ORDER[-1]]

    def copies_of(i):
        low = pltpu.make_async_copy(
            blocks.at[0, i], out_ref.at[:, pl.ds(pl.multiple_of(8 * i, 8), 8), :], sems.at[0, i]
        )
        high = pltpu.make_async_copy(
            blocks.at[1, i], out_ref.at[:, pl.ds(pl.multiple_of(56 - 8 * i, 8), 8), :], sems.at[1, i]
        )
        return low, high

    def layers(i, carry):
        sums_copy(i).wait()
        for k in range(4):
            acc = (sums[4 * i + k] + layer_product(lines, sines, from_group, 8 * i + 2 * k, apart)) * scale
            blocks[0, i, :, 2 * k, :] = acc[:count, :128]
            blocks[0, i, :, 2 * k + 1, :] = acc[:count, 128:]
            mirror = flipped(jnp.concatenate([acc[count:, :128], acc[count:, 128:]], axis=0), flip)
            blocks[1, i, :, 7 - 2 * k, :] = mirror[:count]
            blocks[1, i, :, 6 - 2 * k, :] = mirror[count:]
        for copy in copies_of(i):
            copy.start()
        return carry

    lax.fori_loop(0, 4, layers, 0)

    def finish(i, carry):
        for copy in copies_of(i):
            copy.wait()
        return carry

    lax.fori_loop(0, 4, finish, 0)
    smalls[2].wait()


def whole_kernel(
    groups, angles_hbm, rows_hbm, cols_hbm, defocus_hbm, v_hbm, m_hbm, residual_hbm, sums_hbm, lines_hbm,
    angles, sines, rows, cols, defocus, rows_b, cols_b, rows_v, cols_v, rows_bv, cols_bv, v_ref, measured,
    residual, windows, windows_b, img, back_windows, load_sems, v_sems, note_sems, *rest
):
    project_refs, image_refs, back_refs = rest[:6], rest[6:-6], rest[-6:]
    me, tile = lax.axis_index("tilt"), lax.axis_index("tile")
    rights, lefts, sibling, below, above = ring_devices()
    smalls = [
        pltpu.make_async_copy(src, dst, load_sems.at[k])
        for k, (src, dst) in enumerate((
            (angles_hbm, angles), (rows_hbm, rows_v), (cols_hbm, cols_v), (rows_hbm, rows), (cols_hbm, cols),
            (defocus_hbm, defocus), (m_hbm, measured),
        ))
    ]
    parts = v_sems.shape[0]
    size = v_ref.shape[0] // parts
    loads = []
    for i in range(parts):
        at = pl.ds(i * size, size)
        loads.append(pltpu.make_async_copy(v_hbm.at[at], v_ref.at[at], v_sems.at[i]))
        loads[-1].start()
    for copy in smalls:
        copy.start()
    partners = [((me + d) % groups, tile) for d in range(1, groups)]
    partners += [sibling, below, above, rights[0], rights[1], lefts[0], lefts[1]]
    for device in partners:
        signal(device)
    smalls[0].wait()
    for t in range(sines.shape[0]):
        sines[t] = sine(angles[0, t])
    notes = [
        remote(src, dst, note_sems.at[0, k], note_sems.at[1, k], sibling)
        for k, (src, dst) in enumerate(((rows_v, rows_bv), (cols_v, cols_bv)))
    ]

    def ready():
        pl.semaphore_wait(pltpu.get_barrier_semaphore(), len(partners))
        for k in (1, 2):
            smalls[k].wait()
        for copy in notes:
            copy.start()

    project_part(groups, me, tile, sibling, loads, ready, sines, v_ref, windows, windows_b, *project_refs)
    for copy in notes:
        copy.wait()
    into = [
        pltpu.make_async_copy(src, dst, load_sems.at[7 + k])
        for k, (src, dst) in enumerate(((rows_bv, rows_b), (cols_bv, cols_b)))
    ]
    for copy in into:
        copy.start()
    for copy in smalls[3:] + into:
        copy.wait()
    image_part(defocus, rows, cols, rows_b, cols_b, windows, windows_b, measured, residual, img, *image_refs)
    keep = pltpu.make_async_copy(residual, residual_hbm, load_sems.at[9])
    keep.start()
    got, lines, sums, send_sems, recv_sems, sems = back_refs
    copies = back_copies(groups, me, tile, back_windows, got, send_sems, recv_sems)

    def send(t):
        for (tilt, _), copy in copies.items():
            if tilt == t:
                copy.start()

    cut_part(rows, cols, img, back_windows, send)
    back_part(groups, me, sines, copies, back_windows, sums_hbm, lines_hbm, got, lines, sums, sems)
    keep.wait()


VMEM = pl.BlockSpec(memory_space=pltpu.VMEM)
HBM = pl.BlockSpec(memory_space=pltpu.HBM)


def call_whole(volumes, angles, defocus, rows, cols, measured, groups):
    boxes, slab, depth, width = volumes.shape
    lines = boxes * slab
    dma = lambda *shape: pltpu.SemaphoreType.DMA(shape)
    blocks = lambda *shape: pltpu.VMEM(shape, BF16)
    floats = lambda *shape: pltpu.VMEM(shape, F32)
    count = 2 * boxes * 128
    whole = [
        pltpu.SMEM((1, 2 * groups), F32),
        pltpu.SMEM((2 * groups,), F32),
        pltpu.SMEM((2, boxes), jnp.int32),
        pltpu.SMEM((2, boxes), jnp.int32),
        pltpu.SMEM((1, 2), F32),
        pltpu.SMEM((2, boxes), jnp.int32),
        pltpu.SMEM((2, boxes), jnp.int32),
        pltpu.VMEM((2, boxes), jnp.int32),
        pltpu.VMEM((2, boxes), jnp.int32),
        pltpu.VMEM((2, boxes), jnp.int32),
        pltpu.VMEM((2, boxes), jnp.int32),
        blocks(lines * depth, width),
        floats(*measured.shape),
        floats(*measured.shape),
        blocks(2, boxes, slab * groups, width),
        blocks(2, boxes, slab * groups, width),
        blocks(2, 4096, 256),
        blocks(2, boxes, slab * groups, width),
        dma(10), dma(4), dma(2, 2),
    ]
    project = [
        floats(lines * depth, width),
        blocks(depth // 4, 2 * lines, 2 * width),
        blocks(groups, 2, boxes, slab, width),
        dma(groups), dma(groups), dma(2, groups),
    ]
    image = [
        floats(2, 16, 128),
        pltpu.SMEM((2, 16, 128), F32),
        blocks(2, count, 256),
        blocks(2, 512, count),
        floats(2, 3, 4, 128, 256),
        blocks(2, 3, 4, 128, 256),
        blocks(2, 2, 2, 128, 256),
        blocks(2, 2, 4, 128, 256),
        blocks(2, 3, 128, 256),
        blocks(2, 2, 64, 256),
        blocks(2, 2, 128, 256),
        blocks(2, 9, 256, 256),
        blocks(2, 128, 256),
        floats(2, 160, 256),
        blocks(2, 2, 16, 256),
        floats(2, 2, 8, 256),
        floats(2, 144, 256),
        dma(2, 2, 6), dma(2, 2, 6), dma(2, 5), dma(2, 2, 36),
    ]
    back = [
        blocks(groups, 2, boxes, slab, width),
        blocks(2, 2 * lines, 2 * width),
        floats(16, 2 * lines, 2 * width),
        dma(2, groups), dma(2, groups), dma(5),
    ]
    angles = angles.reshape(1, -1)
    residual, sums, last = pl.pallas_call(
        functools.partial(whole_kernel, groups),
        out_shape=(
            jax.ShapeDtypeStruct(measured.shape, F32),
            jax.ShapeDtypeStruct((16, 2 * lines, 2 * width), F32),
            jax.ShapeDtypeStruct((2, 2 * lines, 2 * width), BF16),
        ),
        in_specs=[HBM] * 6,
        out_specs=(HBM,) * 3,
        scratch_shapes=whole + project + image + back,
        compiler_params=pltpu.CompilerParams(
            collective_id=0, has_side_effects=True, vmem_limit_bytes=56 * MIB
        ),
    )(angles, rows, cols, defocus.reshape(1, -1), volumes.reshape(lines * depth, width), measured)
    residual, step = pl.pallas_call(
        functools.partial(finish_kernel, groups),
        out_shape=(
            jax.ShapeDtypeStruct(measured.shape, F32), jax.ShapeDtypeStruct((lines, depth, width), F32)
        ),
        in_specs=[HBM] * 4,
        out_specs=(HBM,) * 2,
        scratch_shapes=[
            pltpu.SMEM((1, 2 * groups), F32),
            pltpu.SMEM((2 * groups,), F32),
            blocks(2, 2 * lines, 2 * width),
            floats(16, 2 * lines, 2 * width),
            floats(2, 4, lines, 8, width),
            dma(7), dma(2, 4),
        ],
        compiler_params=pltpu.CompilerParams(vmem_limit_bytes=56 * MIB),
    )(angles, last, sums, residual)
    return residual, step.reshape(volumes.shape)


def shards(volumes, angles, defocus, row_offsets, col_offsets, measured):
    return call_whole(
        volumes, angles, defocus, row_offsets.T, col_offsets.T, measured, lax.axis_size("tilt")
    )


def solution(mesh):
    in_specs = (
        P("tile", "tilt", None, None),
        P(),
        P("tilt"),
        P("tile", "tilt"),
        P("tile", "tilt"),
        P("tilt", "tile", None),
    )
    out_specs = (P("tilt", "tile", None), P("tile", "tilt", None, None))
    return jax.shard_map(shards, mesh=mesh, in_specs=in_specs, out_specs=out_specs, check_vma=False)
```

```python
import functools

import jax
import jax.numpy as jnp
from jax import lax
from jax.experimental import pallas as pl
from jax.experimental.pallas import tpu as pltpu
from jax.sharding import PartitionSpec as P

HR = 8
MESH = pl.DeviceIdType.MESH
BF16 = jnp.bfloat16
F32 = jnp.float32
MIB = 1 << 20


def signal(device):
    pl.semaphore_signal(
        pltpu.get_barrier_semaphore(), inc=1, device_id=device, device_id_type=MESH
    )


def remote(src, dst, send_sem, recv_sem, device):
    return pltpu.make_async_remote_copy(
        src_ref=src, dst_ref=dst, send_sem=send_sem, recv_sem=recv_sem,
        device_id=device, device_id_type=MESH,
    )


def offsets_c_minus_x(transposed):
    rows = lax.broadcasted_iota(jnp.int32, (128, 128), 0)
    cols = lax.broadcasted_iota(jnp.int32, (128, 128), 1)
    return ((rows - cols) if transposed else (cols - rows)).astype(F32).astype(BF16)


def sine(x):
    square = x * x
    value = -1.0 / 39916800.0 + square * (1.0 / 6227020800.0)
    for factor in (1.0 / 362880.0, -1.0 / 5040.0, 1.0 / 120.0, -1.0 / 6.0):
        value = factor + square * value
    return x + x * (square * value)


def shear_block(sines, tilt, layer, apart):
    shift = (jnp.asarray(layer, jnp.int32).astype(F32) - 31.5) * sines[tilt]
    tap = shift.astype(jnp.int32).astype(F32)
    tap = jnp.where(tap > shift, tap - 1.0, tap)
    all_of = lambda value: jnp.full((128, 128), value, F32).astype(BF16)
    near = jnp.maximum(0.0, 1.0 - jnp.abs(tap - shift))
    far = jnp.maximum(0.0, 1.0 - jnp.abs(tap + 1.0 - shift))
    zero = jnp.zeros((128, 128), BF16)
    return jnp.where(apart == all_of(tap), all_of(near), jnp.where(apart == all_of(tap + 1.0), all_of(far), zero))


def shear_tile(sines, tilt, layer, apart, transposed):
    make = lambda t, z: shear_block(sines, tilt + t, layer + z, apart)
    if transposed:
        parts = [[make(t, z) for z in range(2)] for t in range(2)]
    else:
        parts = [[make(t, z) for t in range(2)] for z in range(2)]
    return jnp.concatenate([jnp.concatenate(row, axis=1) for row in parts], axis=0)


def flip_matrix():
    rows = lax.broadcasted_iota(jnp.int32, (128, 128), 0)
    cols = lax.broadcasted_iota(jnp.int32, (128, 128), 1)
    return jnp.where(rows + cols == 127, 1.0, 0.0).astype(BF16)


def flipped(x, flip):
    high = x.astype(BF16)
    low = (x - high.astype(F32)).astype(BF16)
    return jnp.dot(
        jnp.concatenate([high, low], axis=1), jnp.concatenate([flip, flip], axis=0), preferred_element_type=F32
    )


def project_part(
    groups, me, tile, sibling, loads, ready, sines, v_ref, out_ref, pair_ref,
    wide, pairs, sent, send_sems, recv_sems, pair_sems,
):
    rows = v_ref.shape[0]
    lines = rows // 64
    parts = len(loads)
    size = rows // parts

    def widen(i, carry):
        at = pl.ds(pl.multiple_of(i * 512, 512), 512)
        wide[at, :] = v_ref[at, :].astype(F32)
        return carry

    for i in range(parts):
        loads[i].wait()
        lax.fori_loop(i * size // 512, (i + 1) * size // 512, widen, 0)
    flip = flip_matrix()

    def gather(k, carry):
        layer = lambda z: wide[pl.ds(z, lines, stride=64), :]
        top = jnp.concatenate([layer(2 * k), layer(2 * k + 1)], axis=1).astype(BF16)
        mirror = jnp.concatenate([layer(63 - 2 * k), layer(62 - 2 * k)], axis=0).astype(BF16)
        mirror = jnp.dot(mirror, flip, preferred_element_type=F32).astype(BF16)
        pairs[k] = jnp.concatenate([top, jnp.concatenate([mirror[:lines], mirror[lines:]], axis=1)], axis=0)
        return carry

    lax.fori_loop(0, 16, gather, 0)
    ready()
    apart = offsets_c_minus_x(False)
    mine = pl.ds(pl.multiple_of(16 * me, 16), 16)

    def windows_of(target):
        acc = jnp.zeros((2 * lines, 256), F32)
        for k in range(16):
            acc = acc + jnp.dot(
                pairs[k], shear_tile(sines, 2 * target, 2 * k, apart, False), preferred_element_type=F32
            )
        mirror = flipped(jnp.concatenate([acc[lines:, :128], acc[lines:, 128:]], axis=0), flip)
        both = (acc[:lines, :128] + mirror[:lines], acc[:lines, 128:] + mirror[lines:])
        return [half.astype(BF16).reshape(lines // 16, 16, 128) for half in both]

    def copy_of(step):
        d = jnp.where(step % 2 == 0, 4 + step // 2, 4 - (step + 1) // 2)
        target = (me + d) % groups
        return target, remote(
            sent.at[step], out_ref.at[:, :, mine, :], send_sems.at[step], recv_sems.at[step], (target, tile)
        )

    def project(step, carry):
        target, copy = copy_of(step)
        both = windows_of(target)
        for t in range(2):
            sent[step, t] = both[t]
        copy.start()
        return carry

    lax.fori_loop(0, groups - 1, project, 0)
    both = windows_of(me)
    for t in range(2):
        out_ref[t, :, mine, :] = both[t]

    def share(slab, k):
        at = pl.ds(pl.multiple_of(16 * slab, 16), 16)
        return remote(
            out_ref.at[:, :, at, :], pair_ref.at[:, :, at, :], pair_sems.at[0, k], pair_sems.at[1, k], sibling
        )

    def came_from(step):
        d = jnp.where(step % 2 == 0, 4 + step // 2, 4 - (step + 1) // 2)
        return (me + groups - d) % groups

    share(me, groups - 1).start()

    def forward(step, carry):
        copy_of(step)[1].wait_recv()
        share(came_from(step), step).start()
        return carry

    lax.fori_loop(0, groups - 1, forward, 0)

    def finish(step, carry):
        copy_of(step)[1].wait_send()
        share(came_from(step), step).wait()
        return carry

    lax.fori_loop(0, groups - 1, finish, 0)
    share(me, groups - 1).wait()


def ring_devices():
    z, tile = lax.axis_index("tilt"), lax.axis_index("tile")
    x, y, c = tile // 8, (tile // 2) % 4, tile % 2

    def dev(dx, dy):
        return (z, ((x + dx) % 4) * 8 + ((y + dy) % 4) * 2 + c)

    right = (dev(1, 0), dev(0, 1))
    left = (dev(3, 0), dev(0, 3))
    sibling = (z, x * 8 + y * 2 + 1 - c)
    return right, left, sibling, (z, (tile + 1) % 32), (z, (tile + 31) % 32)


def image_part(
    defocus, rows_a, cols_a, rows_b, cols_b, win_a, win_b, measured, residual, img, spread_wide, spread,
    shifted, select, loc, s_b, o_b, f_b, s_c, o_c, f_c, table, pred_half, pred, halo, m_halo, res,
    b_sems, c_sems, h_sems, g_sems,
):
    z, tile = lax.axis_index("tilt"), lax.axis_index("tile")
    x, y, c = tile // 8, (tile // 2) % 4, tile % 2
    rights, lefts, sibling, below, above = ring_devices()
    right = lambda axis: rights[axis]
    left = lambda axis: lefts[axis]
    place = (x, y)
    steps = (2, 1, 3, 0)
    m_copies = []
    for k, (device, start) in enumerate(((below, 120), (above, 0))):
        copy = remote(
            measured.at[:, pl.ds(start, 8), :], m_halo.at[k], h_sems.at[0, k], h_sems.at[1, k], device
        )
        copy.start()
        m_copies.append(copy)

    down = lax.broadcasted_iota(jnp.int32, (16, 128), 0).astype(F32)
    along = lax.broadcasted_iota(jnp.int32, (16, 128), 1).astype(F32)
    rho_sq = down * down + along * along
    scale = float(HR * HR)
    for t in range(2):
        spread_wide[t] = jnp.exp(-rho_sq / (2.0 * scale)) * jnp.cos(defocus[0, t] * rho_sq) / scale
    to_scalars = pltpu.make_async_copy(spread_wide, spread, h_sems.at[0, 4])
    to_scalars.start()

    def fill(i, carry):
        lanes = lax.broadcasted_iota(jnp.int32, (16, 256), 1)
        subs = lax.broadcasted_iota(jnp.int32, (16, 256), 0) + i * 16
        apart = jnp.abs(lanes - subs).astype(F32).astype(BF16)
        masks = [apart == jnp.full((16, 256), j, F32).astype(BF16) for j in range(HR + 1)]
        for t in range(2):
            for a in range(HR + 1):
                value = jnp.zeros((16, 256), BF16)
                for j in range(HR + 1):
                    value = jnp.where(masks[j], jnp.full((16, 256), spread[t, a, j], F32).astype(BF16), value)
                table[t, a, pl.ds(pl.multiple_of(i * 16, 16), 16), :] = value
        return carry


    pending = []

    def go(src, dst, sems, t, k, device):
        copy = remote(src, dst, sems.at[0, t, k], sems.at[1, t, k], device)
        copy.start()
        pending.append(copy)
        return copy

    def at_place(t, p, q):
        return (p, q) if t == 0 else (q, p)

    boxes = win_a.shape[1]
    items = [(win_a, rows_a, cols_a, i) for i in range(boxes)] + [(win_b, rows_b, cols_b, i) for i in range(boxes)]
    left_by = lax.broadcasted_iota(jnp.int32, (128, 256), 1) - lax.broadcasted_iota(jnp.int32, (128, 256), 0)
    left_by = left_by.astype(F32).astype(BF16)
    down_by = lax.broadcasted_iota(jnp.int32, (128, 128), 0) - lax.broadcasted_iota(jnp.int32, (128, 128), 1)
    down_by = down_by.astype(F32).astype(BF16)

    def shift_columns(t):
        for i, (windows, _, cols_ref, b) in enumerate(items):
            col = jnp.full((128, 256), cols_ref[t, b].astype(F32), F32).astype(BF16)
            onto = jnp.where(left_by == col, 1.0, 0.0).astype(BF16)
            moved = jnp.dot(windows[t, b], onto, preferred_element_type=F32)
            shifted[t, pl.ds(128 * i, 128), :] = moved.astype(BF16)

    def canvas(t, k):
        p = (place[t] + steps[k]) % 4
        for q in range(4):
            bx, by = at_place(t, p, q)
            top = (bx * 8 + by * 2 + c) * 128
            for i, (_, rows_ref, _, b) in enumerate(items):
                row = jnp.clip(rows_ref[t, b] - top, -128, 128)
                row = jnp.full((128, 128), row.astype(F32), F32).astype(BF16)
                select[t, pl.ds(128 * q, 128), pl.ds(128 * i, 128)] = jnp.where(down_by == row, 1.0, 0.0).astype(BF16)
        return jnp.dot(select[t], shifted[t], preferred_element_type=F32).reshape(4, 128, 256)

    b_in = {}
    for t in range(2):
        shift_columns(t)
        s_b[t, 0] = canvas(t, 0).astype(BF16)
        for h, device in ((0, right(t)), (1, left(t))):
            b_in[t, "opp", h] = go(s_b.at[t, 0, pl.ds(2 * h, 2)], o_b.at[t, h], b_sems, t, h, device)
    for t in range(2):
        for k, h, device in ((1, 1, right(t)), (2, 0, left(t))):
            loc[t, k - 1] = canvas(t, k)
            at = pl.ds(2 * h, 2)
            s_b[t, k, at] = loc[t, k - 1, at].astype(BF16)
            b_in[t, "free", k] = go(s_b.at[t, k, at], f_b.at[t, k - 1, at], b_sems, t, 1 + k, device)
    for t in range(2):
        for k, h, device in ((1, 0, right(t)), (2, 1, left(t))):
            at = pl.ds(2 * h, 2)
            b_in[t, "opp", h].wait_recv()
            s_b[t, k, at] = (loc[t, k - 1, at] + o_b[t, h].astype(F32)).astype(BF16)
            b_in[t, "bound", k] = go(s_b.at[t, k, at], f_b.at[t, k - 1, at], b_sems, t, 3 + k, device)
    for t in range(2):
        loc[t, 2] = canvas(t, 3)
    to_scalars.wait()
    lax.fori_loop(0, 16, fill, 0)
    for t in range(2):
        for k in (1, 2):
            b_in[t, "free", k].wait_recv()
            b_in[t, "bound", k].wait_recv()

    def local_c(t, k, half):
        q = (place[1 - t] + steps[k]) % 4
        at = pl.ds(64 * half, 64)
        return loc[t, 2, q, at, :] + f_b[t, 0, q, at, :].astype(F32) + f_b[t, 1, q, at, :].astype(F32)

    c_in = {}
    for t in range(2):
        for h, device in ((0, right(1 - t)), (1, left(1 - t))):
            at = pl.ds(64 * h, 64)
            s_c[t, 0, at] = local_c(t, 0, h).astype(BF16)
            c_in[t, "opp", h] = go(s_c.at[t, 0, at], o_c.at[t, h], c_sems, t, h, device)
        for k, h, device in ((1, 1, right(1 - t)), (2, 0, left(1 - t))):
            at = pl.ds(64 * h, 64)
            s_c[t, k, at] = local_c(t, k, h).astype(BF16)
            c_in[t, "free", k] = go(s_c.at[t, k, at], f_c.at[t, k - 1, at], c_sems, t, 1 + k, device)
    for t in range(2):
        for k, h, device in ((1, 0, right(1 - t)), (2, 1, left(1 - t))):
            at = pl.ds(64 * h, 64)
            c_in[t, "opp", h].wait_recv()
            s_c[t, k, at] = (local_c(t, k, h) + o_c[t, h].astype(F32)).astype(BF16)
            c_in[t, "bound", k] = go(s_c.at[t, k, at], f_c.at[t, k - 1, at], c_sems, t, 3 + k, device)
    for t in range(2):
        for k in (1, 2):
            c_in[t, "free", k].wait_recv()
            c_in[t, "bound", k].wait_recv()
        total = jnp.concatenate([local_c(t, 3, h) for h in range(2)], axis=0)
        total = total + f_c[t, 0].astype(F32) + f_c[t, 1].astype(F32)
        pred_half[t] = total.astype(BF16)
        pred[t, pl.ds(16, 128), :] = pred_half[t].astype(F32)

    p_copies = []
    for k, (device, start) in enumerate(((below, 112), (above, 0))):
        copy = remote(
            pred_half.at[:, pl.ds(start, 16), :], halo.at[k], h_sems.at[0, 2 + k], h_sems.at[1, 2 + k], device
        )
        copy.start()
        p_copies.append(copy)
    has_above = jnp.where(tile > 0, 1.0, 0.0).astype(F32)
    has_below = jnp.where(tile < 31, 1.0, 0.0).astype(F32)
    for copy in m_copies + p_copies:
        copy.wait_recv()
    for t in range(2):
        pred[t, pl.ds(0, 16), :] = halo[0, t].astype(F32) * has_above
        pred[t, pl.ds(144, 16), :] = halo[1, t].astype(F32) * has_below

    g_in = {}

    def give(t, bx, by, core, rows, k, device):
        top = (bx * 8 + by * 2 + core) * 128 + rows[0]
        where = img.at[t, pl.ds(pl.multiple_of(top, 64), rows[1]), :]
        copy = remote(where, where, g_sems.at[0, t, k], g_sems.at[1, t, k], device)
        copy.start()
        pending.append(copy)
        return copy

    for t in range(2):
        total = jnp.zeros((144, 256), F32)
        for i in range(2 * HR + 1):
            lhs = pred[t, pl.ds(i, 144), :].astype(BF16)
            total = total + jnp.dot(lhs, table[t, abs(i - HR)], preferred_element_type=F32)
        inner = measured[t] - total[8:136]
        residual[t] = inner
        res[t, pl.ds(8, 128), :] = inner.astype(BF16).astype(F32)
        res[t, pl.ds(0, 8), :] = (m_halo[0, t] - total[0:8]).astype(BF16).astype(F32) * has_above
        res[t, pl.ds(136, 8), :] = (m_halo[1, t] - total[136:144]).astype(BF16).astype(F32) * has_below
        total = jnp.zeros((128, 256), F32)
        for i in range(2 * HR + 1):
            lhs = res[t, pl.ds(i, 128), :].astype(BF16)
            total = total + jnp.dot(lhs, table[t, abs(i - HR)], preferred_element_type=F32)
        img[t, pl.ds(pl.multiple_of(tile * 128, 128), 128), :] = total.astype(BF16)
        whole = (0, 128)
        g_in[t, "q", 0] = give(t, x, y, c, whole, 0, right(1 - t))
        g_in[t, "q", 1] = give(t, x, y, c, whole, 1, left(1 - t))
        g_in[t, "p", 0, 0] = give(t, x, y, c, whole, 4, right(t))
        g_in[t, "p", 0, 1] = give(t, x, y, c, whole, 5, left(t))
        g_in[t, "s", 0, 0] = give(t, x, y, c, whole, 20, sibling)

    def spread_block(t, dq, slot):
        q = (place[1 - t] + dq) % 4
        bx, by = at_place(t, place[t], q)
        g_in[t, "p", slot, 0] = give(t, bx, by, c, (0, 128), 4 + 4 * slot, right(t))
        g_in[t, "p", slot, 1] = give(t, bx, by, c, (0, 128), 5 + 4 * slot, left(t))
        g_in[t, "s", 0, slot] = give(t, bx, by, c, (0, 128), 20 + slot, sibling)

    for t in range(2):
        g_in[t, "q", 0].wait_recv()
        bx, by = at_place(t, place[t], (place[1 - t] + 3) % 4)
        g_in[t, "q", 2] = give(t, bx, by, c, (0, 64), 2, right(1 - t))
        g_in[t, "q", 1].wait_recv()
        bx2, by2 = at_place(t, place[t], (place[1 - t] + 1) % 4)
        g_in[t, "q", 3] = give(t, bx2, by2, c, (64, 64), 3, left(1 - t))
        spread_block(t, 3, 1)
        spread_block(t, 1, 2)
    for t in range(2):
        g_in[t, "q", 2].wait_recv()
        g_in[t, "q", 3].wait_recv()
        spread_block(t, 2, 3)

    offsets = (0, 3, 1, 2)
    for slot in range(4):
        for t in range(2):
            q = (place[1 - t] + offsets[slot]) % 4
            for side, (dp, start, device) in enumerate(((3, 0, right(t)), (1, 64, left(t)))):
                g_in[t, "p", slot, side].wait_recv()
                bx, by = at_place(t, (place[t] + dp) % 4, q)
                g_in[t, "f", slot, side] = give(t, bx, by, c, (start, 64), 6 + 4 * slot + side, device)
                g_in[t, "s", 1 + side, slot] = give(t, bx, by, c, (0, 128), 24 + 4 * side + slot, sibling)
    for slot in range(4):
        for t in range(2):
            q = (place[1 - t] + offsets[slot]) % 4
            g_in[t, "f", slot, 0].wait_recv()
            g_in[t, "f", slot, 1].wait_recv()
            bx, by = at_place(t, (place[t] + 2) % 4, q)
            g_in[t, "s", 3, slot] = give(t, bx, by, c, (0, 128), 32 + slot, sibling)
    for slot in range(4):
        for t in range(2):
            for column in range(4):
                g_in[t, "s", column, slot].wait_recv()
    for copy in m_copies + p_copies + pending:
        copy.wait_send()


def cut_part(rows_ref, cols_ref, img, out_ref, send):
    tilts, boxes = out_ref.shape[:2]
    count = img.shape[1] // 128
    apart = lambda n, m: (
        lax.broadcasted_iota(jnp.int32, (n, m), 0) - lax.broadcasted_iota(jnp.int32, (n, m), 1)
    ).astype(F32).astype(BF16)
    down_by, left_by = apart(128, 256), apart(256, 128)
    fill = lambda value, n, m: jnp.full((n, m), value.astype(F32), F32).astype(BF16)
    for t in range(tilts):
        for b in range(boxes):
            row, col = rows_ref[t, b], cols_ref[t, b]
            home = row // 128
            first, second = fill(home, 16, 256), fill(home + 1, 16, 256)

            def choose(strip, both):
                here = fill(strip, 16, 256)
                masks = [first == here] * 8 + [second == here] * 8
                block = [img[t, pl.ds(pl.multiple_of(strip * 128 + 16 * k, 16), 16), :] for k in range(8)] * 2
                return tuple(jnp.where(*three) for three in zip(masks, block, both))

            nothing = (jnp.zeros((16, 256), BF16),) * 16
            rough = jnp.concatenate(lax.fori_loop(0, count, choose, nothing, unroll=2), axis=0)
            pick = jnp.where(down_by == fill(home * 128 - row, 128, 256), 1.0, 0.0).astype(BF16)
            lines = jnp.dot(pick, rough, preferred_element_type=F32).astype(BF16)
            pick = jnp.where(left_by == fill(col, 256, 128), 1.0, 0.0).astype(BF16)
            out_ref[t, b] = jnp.dot(lines, pick, preferred_element_type=F32).astype(BF16)
        send(t)


ORDER = ((0, 1), (7, 2), (6, 3), (5, 4))


def layer_product(lines, sines, groups_of, layer, apart):
    acc = jnp.zeros((lines.shape[1], 256), F32)
    for slot in range(2):
        weights = shear_tile(sines, 2 * groups_of[slot], layer, apart, True)
        acc = acc + jnp.dot(lines[slot], weights, preferred_element_type=F32)
    return acc


def back_copies(groups, me, tile, windows, got, send_sems, recv_sems):
    copies = {}
    for d in (1, 7, 2, 6, 3, 5, 4):
        target = (me + d) % groups
        for t in range(2):
            copies[t, d] = remote(
                windows.at[t, :, pl.ds(pl.multiple_of(16 * target, 16), 16), :], got.at[d, t],
                send_sems.at[t, d], recv_sems.at[t, d], (target, tile),
            )
    return copies


def back_part(groups, me, sines, copies, windows, sums_hbm, lines_hbm, got, lines, sums, sems):
    flip = flip_matrix()
    count = lines.shape[1] // 2
    apart = offsets_c_minus_x(True)

    def take(slot, rows):
        for t in range(2):
            at = pl.ds(128 * t, 128)
            line = rows[t].reshape(count, 128)
            lines[slot, pl.ds(0, count), at] = line
            lines[slot, pl.ds(count, count), at] = jnp.dot(line, flip, preferred_element_type=F32).astype(BF16)

    def out_copy(i):
        at = pl.ds(4 * i, 4)
        return pltpu.make_async_copy(sums.at[at], sums_hbm.at[at], sems.at[i])

    for stage, pair in enumerate(ORDER):
        for slot, d in enumerate(pair):
            if d == 0:
                take(slot, windows[:, :, pl.ds(pl.multiple_of(16 * me, 16), 16), :])
            else:
                for t in range(2):
                    copies[t, d].wait_recv()
                take(slot, got[d])
        if stage == 3:
            break
        from_group = [(me - d + groups) % groups for d in pair]

        def add(i, carry):
            for k in range(4):
                value = layer_product(lines, sines, from_group, 8 * i + 2 * k, apart)
                sums[4 * i + k] = value if stage == 0 else sums[4 * i + k] + value
            if stage == 2:
                out_copy(i).start()
            return carry

        lax.fori_loop(0, 4, add, 0)
    last = pltpu.make_async_copy(lines, lines_hbm, sems.at[4])
    last.start()

    def finish(i, carry):
        out_copy(i).wait()
        return carry

    lax.fori_loop(0, 4, finish, 0)
    last.wait()
    for copy in copies.values():
        copy.wait_send()


def finish_kernel(
    groups, angles_hbm, lines_hbm, sums_hbm, residual_hbm, residual, out_ref,
    angles, sines, lines, sums, blocks, held, load_sems, sems,
):
    me = lax.axis_index("tilt")

    def sums_copy(i):
        at = pl.ds(4 * i, 4)
        return pltpu.make_async_copy(sums_hbm.at[at], sums.at[at], load_sems.at[i])

    smalls = [
        pltpu.make_async_copy(src, dst, load_sems.at[4 + k])
        for k, (src, dst) in enumerate(((angles_hbm, angles), (lines_hbm, lines), (residual_hbm, held)))
    ]
    smalls[0].start()
    smalls[1].start()
    smalls[2].start()
    for i in range(4):
        sums_copy(i).start()
    through = pltpu.make_async_copy(held, residual, load_sems.at[7])
    smalls[0].wait()
    for t in range(sines.shape[0]):
        sines[t] = sine(angles[0, t])
    smalls[1].wait()
    flip = flip_matrix()
    apart = offsets_c_minus_x(True)
    count = lines.shape[1] // 2
    scale = 1.0 / (2 * groups)
    from_group = [(me - d + groups) % groups for d in ORDER[-1]]

    def copies_of(i):
        low = pltpu.make_async_copy(
            blocks.at[0, i], out_ref.at[:, pl.ds(pl.multiple_of(8 * i, 8), 8), :], sems.at[0, i]
        )
        high = pltpu.make_async_copy(
            blocks.at[1, i], out_ref.at[:, pl.ds(pl.multiple_of(56 - 8 * i, 8), 8), :], sems.at[1, i]
        )
        return low, high

    def layers(i, carry):
        sums_copy(i).wait()
        for k in range(4):
            acc = (sums[4 * i + k] + layer_product(lines, sines, from_group, 8 * i + 2 * k, apart)) * scale
            blocks[0, i, :, 2 * k, :] = acc[:count, :128]
            blocks[0, i, :, 2 * k + 1, :] = acc[:count, 128:]
            mirror = flipped(jnp.concatenate([acc[count:, :128], acc[count:, 128:]], axis=0), flip)
            blocks[1, i, :, 7 - 2 * k, :] = mirror[:count]
            blocks[1, i, :, 6 - 2 * k, :] = mirror[count:]
        for copy in copies_of(i):
            copy.start()
        return carry

    smalls[2].wait()
    through.start()
    lax.fori_loop(0, 4, layers, 0)

    def finish(i, carry):
        for copy in copies_of(i):
            copy.wait()
        return carry

    lax.fori_loop(0, 4, finish, 0)
    through.wait()


def whole_kernel(
    groups, angles_hbm, rows_hbm, cols_hbm, defocus_hbm, v_hbm, m_hbm, residual_hbm, sums_hbm, lines_hbm,
    angles, sines, rows, cols, defocus, rows_b, cols_b, rows_v, cols_v, rows_bv, cols_bv, v_ref, measured,
    residual, windows, windows_b, img, back_windows, load_sems, v_sems, note_sems, *rest
):
    project_refs, image_refs, back_refs = rest[:6], rest[6:-6], rest[-6:]
    me, tile = lax.axis_index("tilt"), lax.axis_index("tile")
    rights, lefts, sibling, below, above = ring_devices()
    smalls = [
        pltpu.make_async_copy(src, dst, load_sems.at[k])
        for k, (src, dst) in enumerate((
            (angles_hbm, angles), (rows_hbm, rows_v), (cols_hbm, cols_v), (rows_hbm, rows), (cols_hbm, cols),
            (defocus_hbm, defocus), (m_hbm, measured),
        ))
    ]
    parts = v_sems.shape[0]
    size = v_ref.shape[0] // parts
    loads = []
    for i in range(parts):
        at = pl.ds(i * size, size)
        loads.append(pltpu.make_async_copy(v_hbm.at[at], v_ref.at[at], v_sems.at[i]))
        loads[-1].start()
    for copy in smalls:
        copy.start()
    partners = [((me + d) % groups, tile) for d in range(1, groups)]
    partners += [sibling, below, above, rights[0], rights[1], lefts[0], lefts[1]]
    for device in partners:
        signal(device)
    smalls[0].wait()
    for t in range(sines.shape[0]):
        sines[t] = sine(angles[0, t])
    notes = [
        remote(src, dst, note_sems.at[0, k], note_sems.at[1, k], sibling)
        for k, (src, dst) in enumerate(((rows_v, rows_bv), (cols_v, cols_bv)))
    ]

    def ready():
        pl.semaphore_wait(pltpu.get_barrier_semaphore(), len(partners))
        for k in (1, 2):
            smalls[k].wait()
        for copy in notes:
            copy.start()

    project_part(groups, me, tile, sibling, loads, ready, sines, v_ref, windows, windows_b, *project_refs)
    for copy in notes:
        copy.wait()
    into = [
        pltpu.make_async_copy(src, dst, load_sems.at[7 + k])
        for k, (src, dst) in enumerate(((rows_bv, rows_b), (cols_bv, cols_b)))
    ]
    for copy in into:
        copy.start()
    for copy in smalls[3:] + into:
        copy.wait()
    image_part(defocus, rows, cols, rows_b, cols_b, windows, windows_b, measured, residual, img, *image_refs)
    keep = pltpu.make_async_copy(residual, residual_hbm, load_sems.at[9])
    keep.start()
    got, lines, sums, send_sems, recv_sems, sems = back_refs
    copies = back_copies(groups, me, tile, back_windows, got, send_sems, recv_sems)

    def send(t):
        for (tilt, _), copy in copies.items():
            if tilt == t:
                copy.start()

    cut_part(rows, cols, img, back_windows, send)
    back_part(groups, me, sines, copies, back_windows, sums_hbm, lines_hbm, got, lines, sums, sems)
    keep.wait()


VMEM = pl.BlockSpec(memory_space=pltpu.VMEM)
HBM = pl.BlockSpec(memory_space=pltpu.HBM)


def call_whole(volumes, angles, defocus, rows, cols, measured, groups):
    boxes, slab, depth, width = volumes.shape
    lines = boxes * slab
    dma = lambda *shape: pltpu.SemaphoreType.DMA(shape)
    blocks = lambda *shape: pltpu.VMEM(shape, BF16)
    floats = lambda *shape: pltpu.VMEM(shape, F32)
    count = 2 * boxes * 128
    whole = [
        pltpu.SMEM((1, 2 * groups), F32),
        pltpu.SMEM((2 * groups,), F32),
        pltpu.SMEM((2, boxes), jnp.int32),
        pltpu.SMEM((2, boxes), jnp.int32),
        pltpu.SMEM((1, 2), F32),
        pltpu.SMEM((2, boxes), jnp.int32),
        pltpu.SMEM((2, boxes), jnp.int32),
        pltpu.VMEM((2, boxes), jnp.int32),
        pltpu.VMEM((2, boxes), jnp.int32),
        pltpu.VMEM((2, boxes), jnp.int32),
        pltpu.VMEM((2, boxes), jnp.int32),
        blocks(lines * depth, width),
        floats(*measured.shape),
        floats(*measured.shape),
        blocks(2, boxes, slab * groups, width),
        blocks(2, boxes, slab * groups, width),
        blocks(2, 4096, 256),
        blocks(2, boxes, slab * groups, width),
        dma(10), dma(4), dma(2, 2),
    ]
    project = [
        floats(lines * depth, width),
        blocks(depth // 4, 2 * lines, 2 * width),
        blocks(groups, 2, boxes, slab, width),
        dma(groups), dma(groups), dma(2, groups),
    ]
    image = [
        floats(2, 16, 128),
        pltpu.SMEM((2, 16, 128), F32),
        blocks(2, count, 256),
        blocks(2, 512, count),
        floats(2, 3, 4, 128, 256),
        blocks(2, 3, 4, 128, 256),
        blocks(2, 2, 2, 128, 256),
        blocks(2, 2, 4, 128, 256),
        blocks(2, 3, 128, 256),
        blocks(2, 2, 64, 256),
        blocks(2, 2, 128, 256),
        blocks(2, 9, 256, 256),
        blocks(2, 128, 256),
        floats(2, 160, 256),
        blocks(2, 2, 16, 256),
        floats(2, 2, 8, 256),
        floats(2, 144, 256),
        dma(2, 2, 6), dma(2, 2, 6), dma(2, 5), dma(2, 2, 36),
    ]
    back = [
        blocks(groups, 2, boxes, slab, width),
        blocks(2, 2 * lines, 2 * width),
        floats(16, 2 * lines, 2 * width),
        dma(2, groups), dma(2, groups), dma(5),
    ]
    angles = angles.reshape(1, -1)
    residual, sums, last = pl.pallas_call(
        functools.partial(whole_kernel, groups),
        out_shape=(
            jax.ShapeDtypeStruct(measured.shape, F32),
            jax.ShapeDtypeStruct((16, 2 * lines, 2 * width), F32),
            jax.ShapeDtypeStruct((2, 2 * lines, 2 * width), BF16),
        ),
        in_specs=[HBM] * 6,
        out_specs=(HBM,) * 3,
        scratch_shapes=whole + project + image + back,
        compiler_params=pltpu.CompilerParams(
            collective_id=0, has_side_effects=True, vmem_limit_bytes=56 * MIB
        ),
    )(angles, rows, cols, defocus.reshape(1, -1), volumes.reshape(lines * depth, width), measured)
    residual, step = pl.pallas_call(
        functools.partial(finish_kernel, groups),
        out_shape=(
            jax.ShapeDtypeStruct(measured.shape, F32), jax.ShapeDtypeStruct((lines, depth, width), F32)
        ),
        in_specs=[HBM] * 4,
        out_specs=(HBM,) * 2,
        scratch_shapes=[
            pltpu.SMEM((1, 2 * groups), F32),
            pltpu.SMEM((2 * groups,), F32),
            blocks(2, 2 * lines, 2 * width),
            floats(16, 2 * lines, 2 * width),
            floats(2, 4, lines, 8, width),
            floats(*measured.shape),
            dma(8), dma(2, 4),
        ],
        compiler_params=pltpu.CompilerParams(vmem_limit_bytes=56 * MIB),
    )(angles, last, sums, residual)
    return residual, step.reshape(volumes.shape)


def shards(volumes, angles, defocus, row_offsets, col_offsets, measured):
    return call_whole(
        volumes, angles, defocus, row_offsets.T, col_offsets.T, measured, lax.axis_size("tilt")
    )


def solution(mesh):
    in_specs = (
        P("tile", "tilt", None, None),
        P(),
        P("tilt"),
        P("tile", "tilt"),
        P("tile", "tilt"),
        P("tilt", "tile", None),
    )
    out_specs = (P("tilt", "tile", None), P("tile", "tilt", None, None))
    return jax.shard_map(shards, mesh=mesh, in_specs=in_specs, out_specs=out_specs, check_vma=False)
```
